512 devices in a mesh: ctx: 32 (over y_hi, z), tp: 16 (over x, y_lo, core).
Axes of the slice: x: 4, y: 4 (y_hi: 2, y_lo: 2; y = y_hi * 2 + y_lo), z: 16, core: 2. Of those that a mesh axis runs over, the one named last changes fastest.
Arguments:
- query_proj: bfloat16 [4096, 4096], P('ctx', 'tp'), may hold values from -64 to 64
- key_proj: bfloat16 [4096, 1024], P('ctx'), may hold values from -64 to 64
- value_proj: bfloat16 [4096, 1024], P('ctx'), may hold values from -6 to 6
- residual: bfloat16 [4096, 5120], P('ctx', 'tp'), may hold values from -6 to 6
- out_weight: bfloat16 [4096, 5120], P('tp', 'ctx'), may hold values from -0.1875 to 0.1875
- norm_gain: bfloat16 [5120], P('tp'), may hold values from 0.25 to 1.75
- mlp_weight: bfloat16 [5120, 5120], P('ctx', 'tp'), may hold values from -0.078125 to 0.078125
- level_weight: bfloat16 [5120, 128], P('tp'), may hold values from -0.078125 to 0.078125
- step_positions: int32 [1024], replicated, may hold values from 0 to 4095, as said below
Outputs:
- attended: bfloat16 [4096, 4096], P('ctx', 'tp')
- step_states: bfloat16 [1024, 5120], P('ctx', 'tp')
- step_levels: float32 [1024, 128], P('ctx', 'tp')
The draws below stay inside these ranges and needn't reach their ends.
Inputs may be any that keep to these rules, and one draw needn't show every extreme that they name: `step_positions`: 1024 distinct increasing positions; the 128 rows of one index of ctx hold at most 128 of them, and some index holds exactly that many.
All inputs are finite; a program needn't handle non-finite values.
Results may differ from the reference program's by a relative error of at most 0.013.
Values may be sent and summed in bfloat16 or wider, within the bound.
A program may use at most 64 MiB of HBM per device.

```python
import math
import jax
import jax.numpy as jnp
from jax import lax

D = 5120
KVH = 8
HD = 128
QH = 32
FFD = 5120
NOUT = 128
TOK_DEV = 128
STEPS_DEV = 32
SEQ = 4096
N_CTX = 32


def shared_keys(key):
    return jax.random.normal(key, (SEQ, KVH * HD), jnp.float32)


def draw_key_proj(key, part):
    base_keys = shared_keys(key)
    return jnp.clip(base_keys, -64.0, 64.0).astype(jnp.bfloat16)


def draw_query_proj(key, part):
    key = jax.random.fold_in(key, 5)
    queries = jax.random.normal(key, (SEQ, QH * HD), jnp.float32)
    return jnp.clip(queries, -64.0, 64.0).astype(jnp.bfloat16)


def draw_step_positions(key, part):
    key = jax.random.fold_in(key, 3)
    devices = SEQ // TOK_DEV
    most = 4 * STEPS_DEV
    total = STEPS_DEV * devices
    first_key, second_key, third_key = jax.random.split(key, 3)
    heavy = jax.random.randint(first_key, (), 0, devices)
    spots = jnp.arange(SEQ, dtype=jnp.int32)
    holder = spots // TOK_DEV
    within = spots % TOK_DEV
    shifts = jax.random.randint(third_key, (devices,), 0, TOK_DEV)
    scores = jax.random.permutation(second_key, SEQ).astype(jnp.int32)
    heavy_rows = holder == heavy
    light_rows = jnp.logical_and(jnp.logical_not(heavy_rows), (within - shifts[holder]) % TOK_DEV < most)
    heavy_score = jnp.where(heavy_rows, scores, 2 * SEQ + scores)
    light_score = jnp.where(light_rows, scores, 2 * SEQ + scores)
    unused_a, heavy_pick = lax.top_k(-heavy_score, most)
    unused_b, light_pick = lax.top_k(-light_score, total - most)
    picks = jnp.concatenate([heavy_pick, light_pick]).astype(jnp.int32)
    return jnp.sort(picks).astype(jnp.int32)


def spiked(values, own_key, source, target, shards_of, factor):
    def block_of(dim):
        return (jnp.arange(values.shape[dim]) // (values.shape[dim] // shards_of)).reshape((-1,) + (1,) * (values.ndim - 1 - dim))

    first = jax.random.permutation(own_key, shards_of)[block_of(target)]
    other_side = (block_of(target) + shards_of // 2) % shards_of
    return jnp.where((block_of(source) == first) | (block_of(source) == other_side), factor * values, values)


def levels(key, extent, cuts, low, high):
    level, own = 1.0, jax.random.fold_in(key, 6)
    for dim, blocks in cuts:
        steps = jnp.exp(jax.random.uniform(jax.random.fold_in(own, dim), (blocks,), jnp.float32, low / len(cuts), high / len(cuts)))
        level = level * jnp.repeat(steps, extent[dim] // blocks).reshape([-1 if axis == dim else 1 for axis in range(len(extent))])
    return level


def gaussian(key, shape, scale, limit, cuts=(), kind=jnp.bfloat16):
    array = jax.random.normal(key, shape, jnp.float32) * scale
    if len(cuts) > 0:
        array = levels(key, shape, cuts, -0.22, 0.18) * array
    return jnp.clip(array, min=-limit, max=limit).astype(kind)


def heavy_noise(stream_key, extent, deviation, most, shards, heavy, kind=jnp.bfloat16):
    values = deviation * jax.random.normal(stream_key, extent, jnp.float32)
    if shards:
        values = values * levels(stream_key, extent, shards, -0.22, 0.18)
    return jnp.clip(spiked(values, jax.random.fold_in(stream_key, 3), *heavy), -most, most).astype(kind)


def setup_inputs(seed: int = 0) -> dict:
    key_of = jax.random.split(jax.random.key(seed), 10)
    query_proj = draw_query_proj(jax.random.fold_in(key_of[9], 71), 0)
    key_proj = draw_key_proj(jax.random.fold_in(key_of[9], 71), 0)
    value_proj = gaussian(key_of[2], (SEQ, KVH * HD), 1.0, 6.0, ((0, 32),))
    residual = gaussian(key_of[3], (SEQ, D), 1.0, 6.0, ((0, 32), (1, 16)))
    out_weight = heavy_noise(key_of[4], (QH * HD, D), (QH * HD) ** -0.5, 0.1875, ((0, 16), (1, 32)), (0, 1, 32, 2.75))
    norm_gain = jnp.clip(1.0 + 0.15 * jax.random.normal(key_of[5], (D,), jnp.float32), 0.25, 1.75).astype(jnp.bfloat16)
    mlp_weight = gaussian(key_of[6], (D, FFD), D ** -0.5, 0.078125, ((0, 32), (1, 16)))
    level_weight = gaussian(key_of[7], (FFD, NOUT), FFD ** -0.5, 0.078125, ((0, 16),))
    step_positions = draw_step_positions(jax.random.fold_in(key_of[9], 71), 0)
    return dict(query_proj=query_proj, key_proj=key_proj, value_proj=value_proj, residual=residual, out_weight=out_weight, norm_gain=norm_gain, mlp_weight=mlp_weight, level_weight=level_weight, step_positions=step_positions)


def attend_block(query_block, block_start, key_proj, value_proj):
    width = query_block.shape[0]
    length = key_proj.shape[0]
    group = QH // KVH
    scale = HD ** (-0.5)
    query_spots = block_start + jnp.arange(width, dtype=jnp.int32)
    key_spots = jnp.arange(length, dtype=jnp.int32)
    allowed = key_spots[None, :] <= query_spots[:, None]
    pieces = []
    for head in range(KVH):
        query_part = query_block[:, head * group * HD:(head + 1) * group * HD].reshape(width, group, HD).astype(jnp.float32)
        key_part = key_proj[:, head * HD:(head + 1) * HD].astype(jnp.float32)
        value_part = value_proj[:, head * HD:(head + 1) * HD].astype(jnp.float32)
        scores = jnp.einsum('qgd,pd->gqp', query_part, key_part) * scale
        scores = jnp.where(allowed[None], scores, -1e+30)
        highest = lax.optimization_barrier(jnp.max(scores, axis=-1, keepdims=True))
        weights = jnp.exp(scores - highest)
        totals = lax.optimization_barrier(jnp.sum(weights, axis=-1))
        rounded = lax.optimization_barrier(weights.astype(jnp.bfloat16))
        mixed = jnp.einsum('gqp,pd->gqd', rounded.astype(jnp.float32), value_part) / totals[..., None]
        pieces.append(mixed.transpose(1, 0, 2).reshape(width, group * HD))
    return jnp.concatenate(pieces, axis=1).astype(jnp.bfloat16)

def reference(query_proj, key_proj, value_proj, residual, out_weight, norm_gain, mlp_weight, level_weight, step_positions):
    length = query_proj.shape[0]
    block = math.gcd(length, 1024)
    blocks = length // block
    starts = jnp.arange(blocks, dtype=jnp.int32) * block
    stacked = query_proj.reshape(blocks, block, QH * HD)
    result = lax.map(lambda item: attend_block(item[0], item[1], key_proj, value_proj), (stacked, starts))
    attended = result.reshape(length, QH * HD)
    count = step_positions.shape[0]
    ordinal = jnp.arange(count, dtype=jnp.int32)
    step_order = ordinal % STEPS_DEV * N_CTX + ordinal // STEPS_DEV
    spots = step_positions[step_order]
    projected = jnp.dot(attended[spots], out_weight, preferred_element_type=jnp.float32)
    step_states = (residual[spots].astype(jnp.float32) + projected).astype(jnp.bfloat16)
    states_wide = step_states.astype(jnp.float32)
    meansq = lax.optimization_barrier(jnp.mean(states_wide * states_wide, axis=-1, keepdims=True))
    normed = (states_wide * lax.rsqrt(meansq + 1e-06) * norm_gain.astype(jnp.float32)).astype(jnp.bfloat16)
    pre = jnp.dot(normed, mlp_weight, preferred_element_type=jnp.float32)
    hidden = jax.nn.silu(pre).astype(jnp.bfloat16)
    step_levels = jnp.dot(hidden, level_weight, preferred_element_type=jnp.float32)
    return (attended, step_states, step_levels)
```

```python
import functools

import jax
import jax.numpy as jnp
from jax import lax
from jax.experimental import pallas as pl
from jax.experimental.pallas import tpu as pltpu
from jax.sharding import PartitionSpec as P

D = 5120
HD = 128
TOK = 128
STEPS = 32
COLS = 640
MASKED = -1e30
MESH = pl.DeviceIdType.MESH
F32 = jnp.float32
BF16 = jnp.bfloat16
I32 = jnp.int32
NEAR = (0, -1, 1, -2)


def iota(shape, dim):
    return lax.broadcasted_iota(I32, shape, dim)


def nn(a, b):
    return lax.dot_general(a, b, (((1,), (0,)), ((), ())), preferred_element_type=F32)


def nt(a, b):
    return lax.dot_general(a, b, (((1,), (1,)), ((), ())), preferred_element_type=F32)


def tn(a, b):
    return lax.dot_general(a, b, (((0,), (0,)), ((), ())), preferred_element_type=F32)


def shift(rows, cols, offset):
    return (iota((rows, cols), 0) + offset == iota((rows, cols), 1)).astype(BF16)


def kernel(
    q_ref, k_ref, v_ref, res_ref, wo_ref, gain_ref, wm_ref, lw_ref, pos_ref,
    att_ref, states_ref, levels_ref,
    kv, qall, qsend, qrecv, qmid_s, qmid_r, posc,
    rsend, rbuf, gbuf, wob, wmb, wobig, wmbig, lwt,
    agrp, pb, rb, sb, ob_s, ob, yb, yr, fb, fr,
    far_s, far_r, near_s, near_r, y_s, y_r, c_s, c_r,
    q_s, q_r, qm_s, qm_r, r_s, r_r, g_s, g_r, w_s, w_r,
    a_s, a_r, p_s, p_r, s_s, s_r, o_s, o_r, z_s, z_r, f_s, f_r,
):
    c = lax.axis_index("ctx")
    t = lax.axis_index("tp")
    z = lax.rem(c, 16)
    yh = c // 16
    core = lax.rem(t, 2)
    group = t // 2
    par = lax.rem(z, 2)
    mate_z = z + 1 - 2 * par
    pair = z // 2
    zr = lax.rem(z, 4)
    zq = z // 4
    partner = ((1 - yh) * 16 + z, t)
    other_core = (c, t + 1 - 2 * core)
    sends = []

    def zdev(d):
        return (yh * 16 + lax.rem(z + 16 + d, 16), t)

    def tdev(d):
        return (c, lax.rem(t + d, 16))

    def send(src, dst, ssem, rsem, dev):
        copy = pltpu.make_async_remote_copy(
            src_ref=src, dst_ref=dst, send_sem=ssem, recv_sem=rsem, device_id=dev, device_id_type=MESH
        )
        copy.start()
        sends.append(copy)

    def arrived(dst, rsem):
        pltpu.make_async_copy(dst, dst, rsem).wait()

    barrier = pltpu.get_barrier_semaphore()

    def greet(dev):
        pl.semaphore_signal(barrier, inc=1, device_id=dev, device_id_type=MESH)

    for d in range(1, 16):
        greet(zdev(d))
        greet(tdev(d))
    greet(partner)
    greet(((1 - yh) * 16 + mate_z, t))
    is_self = lax.rem(t, 8) == pair
    for y in range(2):
        for p in range(2):
            for j in range(2):
                dev = (y * 16 + 2 * lax.rem(t, 8) + p, j * 8 + pair)

                @pl.when(jnp.logical_not((dev[0] == c) & (dev[1] == t)))
                def _(dev=dev):
                    greet(dev)

    pos8 = pos_ref[...]
    hi8 = (pos8 >> 6).astype(F32).astype(BF16)
    lo8 = (pos8 & 63).astype(F32).astype(BF16)
    eye128 = shift(128, 128, 0)
    post = (nt(eye128, hi8) * 64.0 + nt(eye128, lo8)).astype(I32)
    base = c * TOK

    def before(limit):
        hits = jnp.where(pos8 < limit, 1.0, 0.0)
        return jnp.sum(jnp.sum(hits, axis=1, keepdims=True), axis=0, keepdims=True).astype(I32)

    first = before(base)
    selq = jnp.zeros((256, TOK), F32)
    selr = jnp.zeros((128, TOK), F32)
    lane_q = iota((128, 256), 1)
    owner_q = ((lane_q >> 3) & 1) * 16 + (lane_q >> 4)
    lane_r = iota((128, 128), 1)
    owner_r = (lane_r >> 6) * 16 + ((lane_r >> 2) & 7) * 2 + ((lane_r >> 5) & 1)
    for a in range(8):
        col = post[:, a : a + 1]
        step = iota((128, 1), 0) + a * 128
        rank = jnp.where((col >= base) & (col < base + TOK), (step - first) >> 5, 1000)
        owner = step & 31
        held = (col == iota((128, TOK), 1) + base).astype(BF16)
        selq += tn(((owner == owner_q) & (rank == (lane_q & 3))).astype(BF16), held)
        selr += tn(((owner == owner_r) & (rank == (lane_r & 3))).astype(BF16), held)
    selq = selq.astype(BF16)
    head_row = (iota((256, 128), 0) >> 2) & 1
    qsend[...] = jnp.where(head_row == 0, nn(selq, q_ref[:, :HD]), nn(selq, q_ref[:, HD:])).astype(BF16)
    rsend[...] = nn(selr.astype(BF16), res_ref[...]).astype(BF16)
    lanes = pl.ds(pl.multiple_of(group * HD, HD), HD)
    kv[core, yh, zr, zq] = jnp.where(core == 0, k_ref[:, lanes], v_ref[:, lanes])
    qall[0:TOK] = q_ref[:, :HD]
    qall[160 : 160 + TOK] = q_ref[:, HD:]

    def rows_of(count, owner):
        pick = ((iota((count, 8), 0) & 31) >> 2 == iota((count, 8), 1)).astype(BF16)
        spread = nn(pick, hi8) * 64.0 + nn(pick, lo8)
        lane = (iota((count, 128), 0) & 3) * 32 + owner
        return jnp.sum(jnp.where(iota((count, 128), 1) == lane, spread, 0.0), axis=1, keepdims=True)

    mine = rows_of(STEPS, c)
    for h in range(2):
        posc[h * 160 : h * 160 + TOK] = iota((TOK, 128), 0) + base
        posc[h * 160 + TOK : (h + 1) * 160] = jnp.broadcast_to(mine.astype(I32), (STEPS, 128))

    pl.semaphore_wait(barrier, jnp.where(is_self, 39, 40))

    here = kv.at[core, yh, zr, zq]
    for f in (2, 1, 3):
        send(here, here, far_s.at[f], far_r.at[f], zdev(4 * f))
    for d in (8, 7, 9, 6, 10, 5, 11, 4, 12, 3, 13, 2, 14, 1, 15):
        zd = lax.rem(z + d, 16)
        send(
            qsend.at[pl.ds(zd * 16, 16)], qrecv.at[pl.ds(z * 16, 16)], q_s.at[d], q_r.at[d], zdev(d)
        )
    qrecv[pl.ds(pl.multiple_of(z * 16, 16), 16)] = qsend[pl.ds(pl.multiple_of(z * 16, 16), 16)]

    def near_block(f):
        block = kv.at[core, yh, zr, lax.rem(zq + 4 - f, 4)]
        if f:
            arrived(block, far_r.at[f])
        for n in (3, 1, 2):
            send(block, block, near_s.at[n, f], near_r.at[n, f], zdev(-NEAR[n]))

    near_block(0)
    half_t = t // 8
    for g in range(4):
        dev = ((g // 2) * 16 + 2 * lax.rem(t, 8) + g % 2, yh * 8 + pair)
        src = rsend.at[pl.ds(g * 32, 32)]
        dst = rbuf.at[half_t, par]
        own = (dev[0] == c) & (dev[1] == t)

        @pl.when(own)
        def _(src=src, dst=dst):
            pltpu.make_async_copy(src, dst, r_r.at[half_t, par]).start()

        @pl.when(jnp.logical_not(own))
        def _(src=src, dst=dst, dev=dev, g=g):
            pltpu.make_async_remote_copy(
                src_ref=src, dst_ref=dst, send_sem=r_s.at[g], recv_sem=r_r.at[half_t, par],
                device_id=dev, device_id_type=MESH,
            ).start()

    gbuf[t] = jnp.broadcast_to(gain_ref[...].astype(F32), (16, 320)).astype(BF16)
    for d in range(1, 16):
        send(gbuf.at[t], gbuf.at[t], g_s.at[d], g_r.at[d], tdev(d))

    for f in (1, 3, 2):
        near_block(f)

    w_here = yh * 2 + par
    for r, dev in (
        (1, (yh * 16 + mate_z, t)),
        (2, partner),
        (3, ((1 - yh) * 16 + mate_z, t)),
    ):
        send(wo_ref, wob.at[w_here], w_s.at[0, r], w_r.at[0, r], dev)
        rows = pl.ds(pl.multiple_of(w_here * 160, 16), 160)
        send(wm_ref, wmb.at[rows], w_s.at[1, r], w_r.at[1, r], dev)
    wob[w_here] = wo_ref[...]
    wmb[pl.ds(pl.multiple_of(w_here * 160, 16), 160)] = wm_ref[...]

    for d in range(1, 16):
        from_z = lax.rem(z + 16 - d, 16)
        arrived(qrecv.at[pl.ds(from_z * 16, 16)], q_r.at[d])
    lane = iota((STEPS, 256), 1)
    for which in range(2):
        o_y = yh if which == 0 else 1 - yh
        spots = rows_of(STEPS, o_y * 16 + z).astype(I32)
        source = spots >> 7
        diagonal = iota((STEPS, STEPS), 0) == iota((STEPS, STEPS), 1)
        source_row = jnp.sum(
            jnp.where(diagonal, source.astype(F32), 0.0), axis=0, keepdims=True
        ).astype(I32)
        earlier = iota((STEPS, STEPS), 1) < iota((STEPS, STEPS), 0)
        rank = jnp.sum(
            jnp.where((source == source_row) & earlier, 1.0, 0.0), axis=1, keepdims=True
        ).astype(I32)
        for h in range(2):
            wanted = (source & 15) * 16 + o_y * 8 + h * 4 + rank
            take = ((wanted == lane) & (source >> 4 == yh)).astype(BF16)
            rows = nn(take, qrecv[...]).astype(BF16)
            if which == 0:
                qall[h * 160 + TOK : (h + 1) * 160] = rows
            else:
                qmid_s[h * STEPS : (h + 1) * STEPS] = rows
    send(qmid_s, qmid_r, qm_s, qm_r, partner)

    queries = None
    state = [jnp.full((320, 1), MASKED, F32), jnp.zeros((320, 1), F32), jnp.zeros((320, HD), F32)]

    def attend(p, n):
        py = yh if p == 0 else 1 - yh
        set_ = lax.rem(zr + 4 + NEAR[n], 4)
        arrived(kv.at[1 - core, py, set_], c_r.at[p, n])
        keys = kv[0, py, set_].reshape(512, HD)
        values = kv[1, py, set_].reshape(512, HD)
        highest, totals, accum = state
        scores = nt(qall[...], keys) * (HD**-0.5)
        kk = iota((320, 512), 1)
        spot = (py * 16 + set_) * TOK + (kk >> 7) * 512 + (kk & 127)
        scores = jnp.where(spot <= posc[:, 0:1], scores, MASKED)
        new = jnp.maximum(highest, jnp.max(scores, axis=1, keepdims=True))
        alpha = jnp.exp(highest - new)
        weights = jnp.exp(scores - new)
        state[0] = new
        state[1] = totals * alpha + jnp.sum(weights, axis=1, keepdims=True)
        state[2] = accum * alpha + nn(weights.astype(BF16), values)

    waiting = None
    for p in range(2):
        for n in range(4):
            py = yh if p == 0 else 1 - yh
            set_ = lax.rem(zr + 4 + NEAR[n], 4)
            bundle = kv.at[core, py, set_]
            if p == 1:
                arrived(bundle, y_r.at[n])
            elif n > 0:
                for f in range(4):
                    from_z = lax.rem(z + 16 + NEAR[n], 16)
                    arrived(kv.at[core, py, set_, lax.rem(from_z // 4 + 4 - f, 4)], near_r.at[n, f])
            if p == 0:
                send(bundle, bundle, y_s.at[n], y_r.at[n], partner)
            send(bundle, bundle, c_s.at[p, n], c_r.at[p, n], other_core)
            if waiting is None:
                arrived(qmid_r, qm_r)
                for h in range(2):
                    rows = slice(h * 160 + TOK, (h + 1) * 160)
                    qall[rows] = (
                        qall[rows].astype(F32) + qmid_r[h * STEPS : (h + 1) * STEPS].astype(F32)
                    ).astype(BF16)
            else:
                attend(*waiting)
            waiting = (p, n)
    attend(*waiting)
    mixed = (state[2] / state[1]).astype(BF16)
    k_rows = pl.ds(pl.multiple_of(pair * STEPS, STEPS), STEPS)
    for h in range(2):
        agrp[k_rows, h * HD : (h + 1) * HD] = mixed[h * 160 + TOK : (h + 1) * 160]

    for d in (4, 3, 5, 2, 6, 1, 7):
        send(agrp.at[k_rows], agrp.at[k_rows], a_s.at[d], a_r.at[d], zdev(2 * d))
    for h in range(2):
        att_ref[:, h * HD : (h + 1) * HD] = mixed[h * 160 : h * 160 + TOK]

    for r in (1, 2, 3):
        slot = (yh if r < 2 else 1 - yh) * 2 + (par if r % 2 == 0 else 1 - par)
        arrived(wob.at[slot], w_r.at[0, r])
        arrived(wmb.at[pl.ds(pl.multiple_of(slot * 160, 16), 160)], w_r.at[1, r])
    big = nn(wob[0], shift(160, COLS, 0))
    for b in range(1, 4):
        big += nn(wob[b], shift(160, COLS, b * 160))
    wobig[...] = big.astype(BF16)
    wmbig[...] = nn(wmb[...], shift(320, 384, 0)).astype(BF16)
    lwt[...] = jnp.zeros_like(lwt)
    lwt[...] = nn(nt(eye128, lw_ref[...]).astype(BF16), shift(320, 384, 0)).astype(BF16)
    for d in range(1, 16):
        src_t = lax.rem(t + 16 - d, 16)
        arrived(gbuf.at[src_t], g_r.at[d])
    gain = nn(gbuf[pair], shift(320, COLS, 0)) + nn(gbuf[8 + pair], shift(320, COLS, 320))
    gain = gain[0:1]
    for j in range(2):
        for s in range(2):
            arrived(rbuf.at[j, s], r_r.at[j, s])
    row = iota((256, 1), 0)
    spots = rows_of(256, yh * 16 + 2 * (iota((256, 128), 0) >> 5) + par).astype(I32)
    step = (row & 31) * 32 + yh * 16 + 2 * (row >> 5) + par
    slot = iota((256, 64), 1)
    from_second = (spots >> 7) - 2 * t
    rank = jnp.where(from_second == 0, step - before(2 * t * TOK), step - before((2 * t + 1) * TOK)) >> 5
    wanted = jnp.where(
        (from_second == 0) | (from_second == 1), from_second * 32 + (row >> 5) * 4 + rank, 1000
    )
    place = (wanted == slot).astype(BF16)
    res_big = nn(rbuf[0].reshape(64, 320), shift(320, COLS, 0)) + nn(
        rbuf[1].reshape(64, 320), shift(320, COLS, 320)
    )
    res_part = nn(place, res_big.astype(BF16))

    for d in range(1, 8):
        from_k = lax.rem(pair + 8 - d, 8)
        arrived(agrp.at[pl.ds(pl.multiple_of(from_k * STEPS, STEPS), STEPS)], a_r.at[d])
    pb[...] = (nn(agrp[...], wobig[...]) + res_part).astype(BF16)
    for d in range(1, 16):
        to_t = lax.rem(t + d, 16)
        send(pb.at[pl.ds(pl.multiple_of(to_t * 16, 16), 16)], rb.at[t], p_s.at[d], p_r.at[d], tdev(d))
    own_rows = pl.ds(pl.multiple_of(t * 16, 16), 16)
    total = pb[own_rows].astype(F32)
    for d in range(1, 16):
        src_t = lax.rem(t + 16 - d, 16)
        arrived(rb.at[src_t], p_r.at[d])
        total += rb[src_t].astype(F32)
    sb[own_rows] = total.astype(BF16)
    for d in range(1, 16):
        send(sb.at[own_rows], sb.at[own_rows], s_s.at[d], s_r.at[d], tdev(d))
    for d in range(1, 16):
        src_t = lax.rem(t + 16 - d, 16)
        arrived(sb.at[pl.ds(pl.multiple_of(src_t * 16, 16), 16)], s_r.at[d])

    states = sb[...].astype(F32)
    squares = jnp.sum(states * states, axis=1, keepdims=True)
    pre = nn((states * gain).astype(BF16), wmbig[...])
    sq_hi = squares.astype(BF16).astype(F32)
    col = iota((256, 384), 1)
    pre = jnp.where(col == 320, sq_hi, jnp.where(col == 321, squares - sq_hi, pre))
    yb[...] = pre.astype(BF16)
    for d in (4, 3, 5, 2, 6, 1, 7):
        to_k = lax.rem(pair + d, 8)
        send(
            yb.at[pl.ds(pl.multiple_of(to_k * STEPS, STEPS), STEPS)], yr.at[pair], z_s.at[d], z_r.at[d], zdev(2 * d)
        )
    out_k = lax.rem(t, 8)
    block = sb[pl.ds(pl.multiple_of(out_k * STEPS, STEPS), STEPS)]
    ob_s[...] = nn(
        block, (iota((COLS, 320), 0) == iota((COLS, 320), 1) + half_t * 320).astype(BF16)
    ).astype(BF16)
    out_dev = (yh * 16 + 2 * out_k + par, half_t * 8 + pair)
    out_own = (out_dev[0] == c) & (out_dev[1] == t)

    @pl.when(out_own)
    def _():
        pltpu.make_async_copy(ob_s, ob, o_r).start()

    @pl.when(jnp.logical_not(out_own))
    def _():
        pltpu.make_async_remote_copy(
            src_ref=ob_s, dst_ref=ob, send_sem=o_s, recv_sem=o_r, device_id=out_dev, device_id_type=MESH
        ).start()

    total = yb[k_rows].astype(F32)
    for d in range(1, 8):
        from_k = lax.rem(pair + 8 - d, 8)
        arrived(yr.at[from_k], z_r.at[d])
        total += yr[from_k].astype(F32)
    col = iota((STEPS, 384), 1)
    squares = jnp.sum(jnp.where((col == 320) | (col == 321), total, 0.0), axis=1, keepdims=True)
    pre = jnp.where(col < 320, total * lax.rsqrt(squares / D + 1e-06), 0.0)
    hidden = (pre / (1.0 + jnp.exp(-pre))).astype(BF16)
    fb[...] = nt(lwt[...], hidden)
    for d in range(1, 16):
        to_t = lax.rem(t + d, 16)
        send(fb.at[pl.ds(pl.multiple_of(to_t * 8, 8), 8)], fr.at[t], f_s.at[d], f_r.at[d], tdev(d))
    arrived(ob, o_r)
    states_ref[...] = ob[...]
    total = fb[pl.ds(pl.multiple_of(t * 8, 8), 8)]
    for d in range(1, 16):
        src_t = lax.rem(t + 16 - d, 16)
        arrived(fr.at[src_t], f_r.at[d])
        total += fr[src_t]
    levels_ref[...] = total

    for copy in sends:
        copy.wait_send()
    for g in range(4):
        dev = ((g // 2) * 16 + 2 * lax.rem(t, 8) + g % 2, yh * 8 + pair)

        @pl.when(jnp.logical_not((dev[0] == c) & (dev[1] == t)))
        def _(g=g):
            arrived(rsend.at[pl.ds(g * 32, 32)], r_s.at[g])

    @pl.when(jnp.logical_not(out_own))
    def _():
        arrived(ob_s, o_s)


def on_device(q, k, v, res, wo, gain, wm, lw, positions):
    vmem = pl.BlockSpec(memory_space=pltpu.VMEM)
    dma = pltpu.SemaphoreType.DMA
    scratch = [
        pltpu.VMEM((2, 2, 4, 4, TOK, HD), BF16),
        pltpu.VMEM((320, HD), BF16),
        pltpu.VMEM((256, HD), BF16),
        pltpu.VMEM((256, HD), BF16),
        pltpu.VMEM((64, HD), BF16),
        pltpu.VMEM((64, HD), BF16),
        pltpu.VMEM((320, 128), I32),
        pltpu.VMEM((128, 320), BF16),
        pltpu.VMEM((2, 2, 32, 320), BF16),
        pltpu.VMEM((16, 16, 320), BF16),
        pltpu.VMEM((4, 256, 160), BF16),
        pltpu.VMEM((COLS, 320), BF16),
        pltpu.VMEM((256, COLS), BF16),
        pltpu.VMEM((COLS, 384), BF16),
        pltpu.VMEM((128, 384), BF16),
        pltpu.VMEM((256, 256), BF16),
        pltpu.VMEM((256, COLS), BF16),
        pltpu.VMEM((16, 16, COLS), BF16),
        pltpu.VMEM((256, COLS), BF16),
        pltpu.VMEM((32, 320), BF16),
        pltpu.VMEM((32, 320), BF16),
        pltpu.VMEM((256, 384), BF16),
        pltpu.VMEM((8, 32, 384), BF16),
        pltpu.VMEM((128, 32), F32),
        pltpu.VMEM((16, 8, 32), F32),
        dma((4,)), dma((4,)), dma((4, 4)), dma((4, 4)), dma((4,)), dma((4,)), dma((2, 4)), dma((2, 4)),
        dma((16,)), dma((16,)), dma(()), dma(()), dma((4,)), dma((2, 2)), dma((16,)), dma((16,)), dma((2, 4)), dma((2, 4)),
        dma((8,)), dma((8,)), dma((16,)), dma((16,)), dma((16,)), dma((16,)), dma(()), dma(()), dma((8,)), dma((8,)), dma((16,)), dma((16,)),
    ]
    attended, states, levels = pl.pallas_call(
        kernel,
        out_shape=(
            jax.ShapeDtypeStruct((TOK, 2 * HD), BF16),
            jax.ShapeDtypeStruct((STEPS, 320), BF16),
            jax.ShapeDtypeStruct((8, STEPS), F32),
        ),
        in_specs=[vmem] * 9,
        out_specs=(vmem, vmem, vmem),
        scratch_shapes=scratch,
        compiler_params=pltpu.CompilerParams(
            collective_id=0, has_side_effects=True, vmem_limit_bytes=40 * 1024 * 1024
        ),
    )(q, k, v, res, wo, gain.reshape(1, -1), wm, lw, positions.reshape(8, 128))
    return attended, states, levels.T


def solution(mesh):
    in_specs = (
        P("ctx", "tp"),
        P("ctx", None),
        P("ctx", None),
        P("ctx", "tp"),
        P("tp", "ctx"),
        P("tp"),
        P("ctx", "tp"),
        P("tp", None),
        P(),
    )
    out_specs = (P("ctx", "tp"), P("ctx", "tp"), P("ctx", "tp"))
    return jax.shard_map(
        on_device, mesh=mesh, in_specs=in_specs, out_specs=out_specs, check_vma=False
    )
```

```python
import functools

import jax
import jax.numpy as jnp
from jax import lax
from jax.experimental import pallas as pl
from jax.experimental.pallas import tpu as pltpu
from jax.sharding import PartitionSpec as P

D = 5120
HD = 128
TOK = 128
STEPS = 32
COLS = 640
MASKED = -1e30
MESH = pl.DeviceIdType.MESH
F32 = jnp.float32
BF16 = jnp.bfloat16
I32 = jnp.int32


def iota(shape, dim):
    return lax.broadcasted_iota(I32, shape, dim)


def nn(a, b):
    return lax.dot_general(a, b, (((1,), (0,)), ((), ())), preferred_element_type=F32)


def nt(a, b):
    return lax.dot_general(a, b, (((1,), (1,)), ((), ())), preferred_element_type=F32)


def tn(a, b):
    return lax.dot_general(a, b, (((0,), (0,)), ((), ())), preferred_element_type=F32)


def shift(rows, cols, offset):
    return (iota((rows, cols), 0) + offset == iota((rows, cols), 1)).astype(BF16)


def kernel(
    q_hbm, k_hbm, v_hbm, res_hbm, wo_hbm, gain_hbm, wm_hbm, lw_hbm, pos_hbm,
    att_ref, states_ref, levels_ref,
    res_ref, gain_ref, lw_ref, pos_ref, kv, qall, qsend, qrecv, qmid_s, qmid_r, posc,
    rsend, rbuf, gbuf, wob, wmb, wmbig, lwt,
    agrp, res_add, pb, px, ph, rb, sb, ob_s, ob_z, ob, yb, yr, fb, fr,
    in_s, far_s, far_r, near_s, near_r, y_s, y_r, c_s, c_r,
    q_s, q_r, qm_s, qm_r, r_s, r_r, g_s, g_r, w_s, w_r,
    a_s, a_r, x_s, x_r, p_s, p_r, s_s, s_r, o_s, o_r, z_s, z_r, f_s, f_r,
):
    c = lax.axis_index("ctx")
    t = lax.axis_index("tp")
    z = lax.rem(c, 16)
    yh = c // 16
    core = lax.rem(t, 2)
    group = t // 2
    par = lax.rem(z, 2)
    mate_z = z + 1 - 2 * par
    pair = z // 2
    zr = lax.rem(z, 4)
    zq = z // 4
    partner = ((1 - yh) * 16 + z, t)
    other_core = (c, t + 1 - 2 * core)
    sends = []

    def zdev(d):
        return (yh * 16 + lax.rem(z + 16 + d, 16), t)

    def tdev(d):
        return (c, lax.rem(t + d, 16))

    def send(src, dst, ssem, rsem, dev):
        copy = pltpu.make_async_remote_copy(
            src_ref=src, dst_ref=dst, send_sem=ssem, recv_sem=rsem, device_id=dev, device_id_type=MESH
        )
        copy.start()
        sends.append(copy)

    def arrived(dst, rsem):
        pltpu.make_async_copy(dst, dst, rsem).wait()

    barrier = pltpu.get_barrier_semaphore()

    def greet(dev):
        pl.semaphore_signal(barrier, inc=1, device_id=dev, device_id_type=MESH)

    for d in range(1, 16):
        greet(zdev(d))
        greet(tdev(d))
    greet(partner)
    greet(((1 - yh) * 16 + mate_z, t))
    half_t, slot_t = t // 8, lax.rem(t, 8)
    res_to = lax.rem(yh + half_t, 2) * 8 + lax.rem(slot_t + 64 - 3 * pair, 8)
    res_pair = lax.rem(3 * (pair + 8 - slot_t), 8)

    def res_dest(g):
        return ((g // 2) * 16 + 2 * slot_t + g % 2, res_to)

    def res_source(j):
        return lax.rem(half_t + j, 2)

    def elsewhere(dev):
        return jnp.logical_not((dev[0] == c) & (dev[1] == t))

    res_peers = [res_dest(g) for g in range(4)] + [
        (res_source(j) * 16 + 2 * res_pair + p, j * 8 + pair) for j in range(2) for p in range(2)
    ]
    n_peers = 32
    for dev in res_peers:
        n_peers += jnp.where(elsewhere(dev), 1, 0)

        @pl.when(elsewhere(dev))
        def _(dev=dev):
            greet(dev)

    w_here = yh * 2 + par
    wo_rows = pl.ds(pl.multiple_of(w_here * 160, 16), 160)
    lanes = pl.ds(pl.multiple_of(group * HD, HD), HD)
    here = kv.at[core, yh, zr, zq]
    fetches = [
        pltpu.make_async_copy(pos_hbm, pos_ref, in_s.at[0]),
        pltpu.make_async_copy(q_hbm.at[:, pl.ds(0, HD)], qall.at[pl.ds(0, TOK)], in_s.at[1]),
        pltpu.make_async_copy(q_hbm.at[:, pl.ds(HD, HD)], qall.at[pl.ds(160, TOK)], in_s.at[2]),
        pltpu.make_async_copy(res_hbm, res_ref, in_s.at[3]),
        pltpu.make_async_copy(gain_hbm, gain_ref, in_s.at[4]),
        pltpu.make_async_copy(lw_hbm, lw_ref, in_s.at[5]),
        pltpu.make_async_copy(wo_hbm, wob.at[wo_rows], in_s.at[6]),
        pltpu.make_async_copy(wm_hbm, wmb.at[wo_rows], in_s.at[7]),
    ]

    @pl.when(core == 0)
    def _():
        pltpu.make_async_copy(k_hbm.at[:, lanes], here, in_s.at[8]).start()

    @pl.when(core == 1)
    def _():
        pltpu.make_async_copy(v_hbm.at[:, lanes], here, in_s.at[8]).start()

    for fetch in fetches:
        fetch.start()

    fetches[0].wait()
    pos8 = pos_ref[...]
    hi8 = (pos8 >> 6).astype(F32).astype(BF16)
    lo8 = (pos8 & 63).astype(F32).astype(BF16)
    eye128 = shift(128, 128, 0)
    post = (nt(eye128, hi8) * 64.0 + nt(eye128, lo8)).astype(I32)
    base = c * TOK

    def before(limit):
        hits = jnp.where(pos8 < limit, 1.0, 0.0)
        return jnp.sum(jnp.sum(hits, axis=1, keepdims=True), axis=0, keepdims=True).astype(I32)

    first = before(base)
    selq = jnp.zeros((256, TOK), F32)
    selr = jnp.zeros((128, TOK), F32)
    lane_q = iota((128, 256), 1)
    owner_q = ((lane_q >> 3) & 1) * 16 + (lane_q >> 4)
    lane_r = iota((128, 128), 1)
    owner_r = (lane_r >> 6) * 16 + ((lane_r >> 2) & 7) * 2 + ((lane_r >> 5) & 1)
    for a in range(8):
        col = post[:, a : a + 1]
        step = iota((128, 1), 0) + a * 128
        rank = jnp.where((col >= base) & (col < base + TOK), (step - first) >> 5, 1000)
        owner = step & 31
        held = (col == iota((128, TOK), 1) + base).astype(BF16)
        selq += tn(((owner == owner_q) & (rank == (lane_q & 3))).astype(BF16), held)
        selr += tn(((owner == owner_r) & (rank == (lane_r & 3))).astype(BF16), held)
    selq = selq.astype(BF16)
    head_row = (iota((256, 128), 0) >> 2) & 1
    fetches[1].wait()
    fetches[2].wait()
    qsend[...] = jnp.where(
        head_row == 0, nn(selq, qall[0:TOK]), nn(selq, qall[160 : 160 + TOK])
    ).astype(BF16)

    def rows_of(count, owner):
        pick = ((iota((count, 8), 0) & 31) >> 2 == iota((count, 8), 1)).astype(BF16)
        spread = nn(pick, hi8) * 64.0 + nn(pick, lo8)
        lane = (iota((count, 128), 0) & 3) * 32 + owner
        return jnp.sum(jnp.where(iota((count, 128), 1) == lane, spread, 0.0), axis=1, keepdims=True)

    mine = rows_of(STEPS, c)
    for h in range(2):
        posc[h * 160 : h * 160 + TOK] = iota((TOK, 128), 0) + base
        posc[h * 160 + TOK : (h + 1) * 160] = jnp.broadcast_to(mine.astype(I32), (STEPS, 128))

    pl.semaphore_wait(barrier, n_peers)

    arrived(here, in_s.at[8])

    def kv_block(plane, n, f):
        py = yh if plane == 0 else 1 - yh
        from_z = lax.rem(z + (0, 15, 1, 14)[n] + 16 - 4 * f, 16)
        return kv.at[core, py, lax.rem(from_z, 4), from_z // 4]

    def kv_bundle(plane, n, kind):
        py = yh if plane == 0 else 1 - yh
        return kv.at[kind, py, lax.rem(zr + (0, 3, 1, 2)[n], 4)]

    def kv_pass(plane, f):
        block = kv_block(plane, 0, f)
        if plane == 0:
            if f in (0, 1):
                send(block, block, near_s.at[0, 3, f], near_r.at[0, 3, f], zdev(2))
            if f in (0, 3):
                send(block, block, near_s.at[0, 3, 2 + f // 3], near_r.at[0, 3, 2 + f // 3], zdev(-2))
        for n, d in ((1, 1), (2, -1)):
            send(block, block, near_s.at[plane, n, f], near_r.at[plane, n, f], zdev(d))

    def kv_cross(n, f):
        block = kv_block(0, n, f)
        send(block, block, y_s.at[n // 3, f], y_r.at[n // 3, f], partner)

    def kv_core(plane, n):
        bundle = kv_bundle(plane, n, core)
        send(bundle, bundle, c_s.at[plane, n], c_r.at[plane, n], other_core)

    def weight_rows(r):
        slot = (yh if r < 2 else 1 - yh) * 2 + (par if r % 2 == 0 else 1 - par)
        return pl.ds(pl.multiple_of(slot * 160, 16), 160)

    def weight_send(w, r):
        buffer = (wob, wmb)[w]
        rows = weight_rows(1) if r == 3 else wo_rows
        dev = (yh * 16 + mate_z, t) if r == 1 else partner
        send(buffer.at[rows], buffer.at[rows], w_s.at[w, r], w_r.at[w, r], dev)

    def weight_wait(w, r):
        arrived((wob, wmb)[w].at[weight_rows(r)], w_r.at[w, r])

    for f in (2, 1, 3):
        send(here, here, far_s.at[f], far_r.at[f], zdev(4 * f))
    kv_cross(0, 0)
    for d in (8, 7, 9, 6, 10, 5, 11, 4, 12, 3, 13, 2, 14, 1, 15):
        zd = lax.rem(z + d, 16)
        send(
            qsend.at[pl.ds(zd * 16, 16)], qrecv.at[pl.ds(z * 16, 16)], q_s.at[d], q_r.at[d], zdev(d)
        )
    qrecv[pl.ds(pl.multiple_of(z * 16, 16), 16)] = qsend[pl.ds(pl.multiple_of(z * 16, 16), 16)]
    kv_pass(0, 0)
    fetches[6].wait()
    weight_send(0, 2)
    weight_send(0, 1)
    fetches[3].wait()
    rsend[...] = nt(selr.astype(BF16), res_ref[...]).astype(BF16)
    fetches[4].wait()
    gbuf[t] = jnp.broadcast_to(gain_ref[...].astype(F32).reshape(1, 320), (16, 320)).astype(BF16)
    for d in range(1, 16):
        send(gbuf.at[t], gbuf.at[t], g_s.at[d], g_r.at[d], tdev(d))
    fetches[5].wait()
    lwt[...] = nn(nt(eye128, lw_ref[...]).astype(BF16), shift(320, 384, 0)).astype(BF16)

    arrived(kv_block(1, 0, 0), y_r.at[0, 0])
    kv_pass(1, 0)
    for f in (1, 3, 2):
        arrived(kv_block(0, 0, f), far_r.at[f])
        kv_cross(0, f)
        kv_pass(0, f)
    kv_core(0, 0)
    weight_wait(0, 1)
    weight_send(0, 3)

    for d in range(1, 16):
        from_z = lax.rem(z + 16 - d, 16)
        arrived(qrecv.at[pl.ds(from_z * 16, 16)], q_r.at[d])
    lane = iota((STEPS, 256), 1)
    for which in range(2):
        o_y = yh if which == 0 else 1 - yh
        spots = rows_of(STEPS, o_y * 16 + z).astype(I32)
        source = spots >> 7
        diagonal = iota((STEPS, STEPS), 0) == iota((STEPS, STEPS), 1)
        source_row = jnp.sum(
            jnp.where(diagonal, source.astype(F32), 0.0), axis=0, keepdims=True
        ).astype(I32)
        earlier = iota((STEPS, STEPS), 1) < iota((STEPS, STEPS), 0)
        rank = jnp.sum(
            jnp.where((source == source_row) & earlier, 1.0, 0.0), axis=1, keepdims=True
        ).astype(I32)
        for h in range(2):
            wanted = (source & 15) * 16 + o_y * 8 + h * 4 + rank
            take = ((wanted == lane) & (source >> 4 == yh)).astype(BF16)
            rows = nn(take, qrecv[...]).astype(BF16)
            if which == 0:
                qall[h * 160 + TOK : (h + 1) * 160] = rows
            else:
                qmid_s[h * STEPS : (h + 1) * STEPS] = rows
    send(qmid_s, qmid_r, qm_s, qm_r, partner)

    state = [jnp.full((320, 1), MASKED, F32), jnp.zeros((320, 1), F32), jnp.zeros((320, HD), F32)]

    def attend(p, n):
        py = yh if p == 0 else 1 - yh
        set_ = lax.rem(zr + (0, 3, 1, 2)[n], 4)
        arrived(kv_bundle(p, n, 1 - core), c_r.at[p, n])
        keys = kv[0, py, set_].reshape(512, HD)
        values = kv[1, py, set_].reshape(512, HD)
        highest, totals, accum = state
        scores = nt(qall[...], keys) * (HD**-0.5)
        kk = iota((320, 512), 1)
        spot = (py * 16 + set_) * TOK + (kk >> 7) * 512 + (kk & 127)
        scores = jnp.where(spot <= posc[:, 0:1], scores, MASKED)
        new = jnp.maximum(highest, jnp.max(scores, axis=1, keepdims=True))
        alpha = jnp.exp(highest - new)
        weights = jnp.exp(scores - new)
        state[0] = new
        state[1] = totals * alpha + jnp.sum(weights, axis=1, keepdims=True)
        state[2] = accum * alpha + nn(weights.astype(BF16), values)

    for f in (1, 3, 2):
        arrived(kv_block(1, 0, f), y_r.at[0, f])
        kv_pass(1, f)
    kv_core(1, 0)
    arrived(qmid_r, qm_r)
    for h in range(2):
        rows = slice(h * 160 + TOK, (h + 1) * 160)
        qall[rows] = (
            qall[rows].astype(F32) + qmid_r[h * STEPS : (h + 1) * STEPS].astype(F32)
        ).astype(BF16)
    for i, f in ((0, 0), (2, 3), (1, 1), (3, 2)):
        arrived(kv_block(0, 3, f), near_r.at[0, 3, i])
        kv_cross(3, f)
    kv_core(0, 3)
    for g in range(4):
        src = rsend.at[pl.ds(g * 32, 32)]
        dst = rbuf.at[half_t, par]

        @pl.when(jnp.logical_not(elsewhere(res_dest(g))))
        def _(src=src, dst=dst):
            pltpu.make_async_copy(src, dst, r_r.at[half_t, par]).start()

        @pl.when(elsewhere(res_dest(g)))
        def _(src=src, dst=dst, g=g):
            pltpu.make_async_remote_copy(
                src_ref=src, dst_ref=dst, send_sem=r_s.at[g], recv_sem=r_r.at[half_t, par],
                device_id=res_dest(g), device_id_type=MESH,
            ).start()

    attend(0, 0)
    for n in (1, 2):
        for f in range(4):
            arrived(kv_block(0, n, f), near_r.at[0, n, f])
        kv_core(0, n)
    attend(1, 0)
    attend(0, 3)
    for n in (1, 2):
        for f in range(4):
            arrived(kv_block(1, n, f), near_r.at[1, n, f])
        kv_core(1, n)

    for bundle in ((0, 1), (0, 2), (1, 1)):
        attend(*bundle)
    for f in range(4):
        arrived(kv_block(1, 3, f), y_r.at[1, f])
    kv_core(1, 3)
    attend(1, 2)
    attend(1, 3)
    mixed = (state[2] / state[1]).astype(BF16)
    k_rows = pl.ds(pl.multiple_of(pair * STEPS, STEPS), STEPS)
    for h in range(2):
        agrp[k_rows, h * HD : (h + 1) * HD] = mixed[h * 160 + TOK : (h + 1) * 160]

    for d in (4, 3, 5, 2, 6, 1, 7):
        send(agrp.at[k_rows], agrp.at[k_rows], a_s.at[d], a_r.at[d], zdev(2 * d))
    for h in range(2):
        att_ref[:, h * HD : (h + 1) * HD] = mixed[h * 160 : h * 160 + TOK]

    for d in range(1, 16):
        src_t = lax.rem(t + 16 - d, 16)
        arrived(gbuf.at[src_t], g_r.at[d])
    gain = nn(gbuf[pair], shift(320, COLS, 0)) + nn(gbuf[8 + pair], shift(320, COLS, 320))
    gain = gain[0:1]
    for j in range(2):
        for s in range(2):
            arrived(rbuf.at[j, s], r_r.at[j, s])
    row = iota((256, 1), 0)
    spots = rows_of(256, yh * 16 + 2 * (iota((256, 128), 0) >> 5) + par).astype(I32)
    step = (row & 31) * 32 + yh * 16 + 2 * (row >> 5) + par
    slot = iota((256, 64), 1)
    res_part = jnp.zeros((256, COLS), F32)
    for j in range(2):
        source = res_source(j) * 16 + 2 * res_pair
        nth = (spots >> 7) - source
        rank = (step - jnp.where(nth == 0, before(source * TOK), before((source + 1) * TOK))) >> 5
        wanted = jnp.where((nth == 0) | (nth == 1), nth * 32 + (row >> 5) * 4 + rank, 1000)
        rows = nn((wanted == slot).astype(BF16), rbuf[j].reshape(64, 320)).astype(BF16)
        res_part += nn(rows, shift(320, COLS, j * 320))

    res_add[...] = res_part

    weight_wait(0, 2)
    weight_wait(0, 3)
    for d in range(1, 8):
        from_k = lax.rem(pair + 8 - d, 8)
        arrived(agrp.at[pl.ds(pl.multiple_of(from_k * STEPS, STEPS), STEPS)], a_r.at[d])
    mine = pl.ds(pl.multiple_of(core * 128, 128), 128)
    theirs = pl.ds(pl.multiple_of((1 - core) * 128, 128), 128)
    chip = t // 2
    pb[...] = (nt(agrp[theirs], wob[...]) + res_add[theirs]).astype(BF16)
    send(pb, px, x_s.at[0], x_r.at[0], other_core)
    partial = nt(agrp[mine], wob[...]) + res_add[mine]
    arrived(px, x_r.at[0])
    ph[...] = (partial + px[...].astype(F32)).astype(BF16)

    def chip_rows(index):
        return pl.ds(pl.multiple_of(index * 16, 16), 16)

    for d in (4, 3, 5, 2, 6, 1, 7):
        send(ph.at[chip_rows(lax.rem(chip + d, 8))], rb.at[chip], p_s.at[d], p_r.at[d], tdev(2 * d))
    fetches[7].wait()
    weight_send(1, 1)
    weight_send(1, 2)
    total = ph[chip_rows(chip)].astype(F32)
    for d in range(1, 8):
        src = lax.rem(chip + 8 - d, 8)
        arrived(rb.at[src], p_r.at[d])
        total += rb[src].astype(F32)
    own_rows = chip_rows(core * 8 + chip)
    sb[own_rows] = total.astype(BF16)
    for d in (4, 3, 5, 2, 6, 1, 7):
        send(sb.at[own_rows], sb.at[own_rows], s_s.at[d], s_r.at[d], tdev(2 * d))
    weight_wait(1, 1)
    weight_send(1, 3)
    weight_wait(1, 2)
    for d in range(1, 8):
        arrived(sb.at[chip_rows(core * 8 + lax.rem(chip + 8 - d, 8))], s_r.at[d])
    send(sb.at[mine], sb.at[mine], x_s.at[1], x_r.at[1], other_core)
    weight_wait(1, 3)
    wmbig[...] = nn(wmb[...], shift(320, 384, 0)).astype(BF16)

    def score(rows, first_owner):
        states = sb[rows].astype(F32)
        squares = jnp.sum(states * states, axis=1, keepdims=True)
        pre = nn((states * gain).astype(BF16), wmbig[...])
        sq_hi = squares.astype(BF16).astype(F32)
        col = iota((128, 384), 1)
        pre = jnp.where(col == 320, sq_hi, jnp.where(col == 321, squares - sq_hi, pre))
        yb[rows] = pre.astype(BF16)
        for m in range(4):
            k = first_owner + m
            piece = yb.at[pl.ds(pl.multiple_of(k * STEPS, STEPS), STEPS)]

            @pl.when(k != pair)
            def _(k=k, piece=piece):
                pltpu.make_async_remote_copy(
                    src_ref=piece, dst_ref=yr.at[pair], send_sem=z_s.at[k], recv_sem=z_r.at[pair],
                    device_id=(yh * 16 + 2 * k + par, t), device_id_type=MESH,
                ).start()

    score(mine, core * 4)
    arrived(sb.at[theirs], x_r.at[1])
    score(theirs, (1 - core) * 4)

    out_k = lax.rem(slot_t + 3 * pair, 8)
    block = sb[pl.ds(pl.multiple_of(out_k * STEPS, STEPS), STEPS)]
    ob_s[...] = nn(
        block, (iota((COLS, 320), 0) == iota((COLS, 320), 1) + half_t * 320).astype(BF16)
    ).astype(BF16)

    def out_send(src, dst, n, dev):
        @pl.when(elsewhere(dev))
        def _():
            pltpu.make_async_remote_copy(
                src_ref=src, dst_ref=dst, send_sem=o_s.at[n], recv_sem=o_r.at[n], device_id=dev, device_id_type=MESH
            ).start()

        @pl.when(jnp.logical_not(elsewhere(dev)))
        def _():
            pltpu.make_async_copy(src, dst, o_r.at[n]).start()

    out_z = (yh * 16 + 2 * out_k + par, t)
    out_t = (c, half_t * 8 + lax.rem(3 * (pair + 8 - slot_t), 8))
    out_send(ob_s, ob_z, 0, out_z)

    yr[pair] = yb[k_rows]
    for k in range(8):

        @pl.when(k != pair)
        def _(k=k):
            arrived(yr.at[k], z_r.at[k])

    total = yr[0].astype(F32)
    for k in range(1, 8):
        total += yr[k].astype(F32)
    col = iota((STEPS, 384), 1)
    squares = jnp.sum(jnp.where((col == 320) | (col == 321), total, 0.0), axis=1, keepdims=True)
    pre = jnp.where(col < 320, total * lax.rsqrt(squares / D + 1e-06), 0.0)
    arrived(ob_z, o_r.at[0])
    out_send(ob_z, ob, 1, out_t)
    hidden = (pre / (1.0 + jnp.exp(-pre))).astype(BF16)
    fb[...] = nt(lwt[...], hidden)
    for d in range(1, 16):
        to_t = lax.rem(t + d, 16)
        send(fb.at[pl.ds(pl.multiple_of(to_t * 8, 8), 8)], fr.at[t], f_s.at[d], f_r.at[d], tdev(d))
    arrived(ob, o_r.at[1])
    states_ref[...] = ob[...]
    total = fb[pl.ds(pl.multiple_of(t * 8, 8), 8)]
    for d in range(1, 16):
        src_t = lax.rem(t + 16 - d, 16)
        arrived(fr.at[src_t], f_r.at[d])
        total += fr[src_t]
    levels_ref[...] = total

    for copy in sends:
        copy.wait_send()
    for g in range(4):

        @pl.when(elsewhere(res_dest(g)))
        def _(g=g):
            arrived(rsend.at[pl.ds(g * 32, 32)], r_s.at[g])

    for k in range(8):

        @pl.when(k != pair)
        def _(k=k):
            arrived(yr.at[k], z_s.at[k])

    for n, dev in enumerate((out_z, out_t)):

        @pl.when(elsewhere(dev))
        def _(n=n):
            arrived(ob, o_s.at[n])


def on_device(q, k, v, res, wo, gain, wm, lw, positions):
    vmem = pl.BlockSpec(memory_space=pltpu.VMEM)
    dma = pltpu.SemaphoreType.DMA
    scratch = [
        pltpu.VMEM((320, TOK), BF16),
        pltpu.VMEM((320,), BF16),
        pltpu.VMEM((320, 128), BF16),
        pltpu.VMEM((8, 128), I32),
        pltpu.VMEM((2, 2, 4, 4, TOK, HD), BF16),
        pltpu.VMEM((320, HD), BF16),
        pltpu.VMEM((256, HD), BF16),
        pltpu.VMEM((256, HD), BF16),
        pltpu.VMEM((64, HD), BF16),
        pltpu.VMEM((64, HD), BF16),
        pltpu.VMEM((320, 128), I32),
        pltpu.VMEM((128, 320), BF16),
        pltpu.VMEM((2, 2, 32, 320), BF16),
        pltpu.VMEM((16, 16, 320), BF16),
        pltpu.VMEM((COLS, 256), BF16),
        pltpu.VMEM((COLS, 320), BF16),
        pltpu.VMEM((COLS, 384), BF16),
        pltpu.VMEM((128, 384), BF16),
        pltpu.VMEM((256, 256), BF16),
        pltpu.VMEM((256, COLS), F32),
        pltpu.VMEM((128, COLS), BF16),
        pltpu.VMEM((128, COLS), BF16),
        pltpu.VMEM((128, COLS), BF16),
        pltpu.VMEM((8, 16, COLS), BF16),
        pltpu.VMEM((256, COLS), BF16),
        pltpu.VMEM((32, 320), BF16),
        pltpu.VMEM((32, 320), BF16),
        pltpu.VMEM((32, 320), BF16),
        pltpu.VMEM((256, 384), BF16),
        pltpu.VMEM((8, 32, 384), BF16),
        pltpu.VMEM((128, 32), F32),
        pltpu.VMEM((16, 8, 32), F32),
        dma((9,)), dma((4,)), dma((4,)), dma((2, 4, 4)), dma((2, 4, 4)), dma((2, 4)), dma((2, 4)), dma((2, 4)), dma((2, 4)),
        dma((16,)), dma((16,)), dma(()), dma(()), dma((4,)), dma((2, 2)), dma((16,)), dma((16,)), dma((2, 4)), dma((2, 4)),
        dma((8,)), dma((8,)), dma((2,)), dma((2,)), dma((8,)), dma((8,)), dma((8,)), dma((8,)), dma((2,)), dma((2,)), dma((8,)), dma((8,)), dma((16,)), dma((16,)),
    ]
    attended, states, levels = pl.pallas_call(
        kernel,
        out_shape=(
            jax.ShapeDtypeStruct((TOK, 2 * HD), BF16),
            jax.ShapeDtypeStruct((STEPS, 320), BF16),
            jax.ShapeDtypeStruct((8, STEPS), F32),
        ),
        in_specs=[pl.BlockSpec(memory_space=pltpu.HBM)] * 9,
        out_specs=(vmem, vmem, vmem),
        scratch_shapes=scratch,
        compiler_params=pltpu.CompilerParams(
            collective_id=0, has_side_effects=True, vmem_limit_bytes=56 * 1024 * 1024
        ),
    )(q, k, v, res.T, wo.T, gain, wm, lw, positions.reshape(8, 128))
    return attended, states, levels.T


def solution(mesh):
    in_specs = (
        P("ctx", "tp"),
        P("ctx", None),
        P("ctx", None),
        P("ctx", "tp"),
        P("tp", "ctx"),
        P("tp"),
        P("ctx", "tp"),
        P("tp", None),
        P(),
    )
    out_specs = (P("ctx", "tp"), P("ctx", "tp"), P("ctx", "tp"))
    return jax.shard_map(
        on_device, mesh=mesh, in_specs=in_specs, out_specs=out_specs, check_vma=False
    )
```

```python
import functools

import jax
import jax.numpy as jnp
from jax import lax
from jax.experimental import pallas as pl
from jax.experimental.pallas import tpu as pltpu
from jax.sharding import PartitionSpec as P

D = 5120
HD = 128
TOK = 128
STEPS = 32
COLS = 640
MASKED = -1e30
MESH = pl.DeviceIdType.MESH
F32 = jnp.float32
BF16 = jnp.bfloat16
I32 = jnp.int32


def iota(shape, dim):
    return lax.broadcasted_iota(I32, shape, dim)


def nn(a, b):
    return lax.dot_general(a, b, (((1,), (0,)), ((), ())), preferred_element_type=F32)


def nt(a, b):
    return lax.dot_general(a, b, (((1,), (1,)), ((), ())), preferred_element_type=F32)


def tn(a, b):
    return lax.dot_general(a, b, (((0,), (0,)), ((), ())), preferred_element_type=F32)


def shift(rows, cols, offset):
    return (iota((rows, cols), 0) + offset == iota((rows, cols), 1)).astype(BF16)


def kernel(
    q_hbm, k_hbm, v_hbm, res_hbm, wo_hbm, gain_hbm, wm_hbm, lw_hbm, pos_hbm,
    att_ref, states_ref, levels_ref,
    res_ref, gain_ref, lw_ref, pos_ref, kv, qall, qsend, qrecv, qmid_s, qmid_r, posc,
    rsend, rmid, rbuf, gbuf, wob, wmb, wmbig, lwt,
    agrp, res_add, pb, px, ph, rb, sb, ob_s, ob_z, ob, yb, yr, fb, fr,
    in_s, far_s, far_r, near_s, near_r, y_s, y_r, c_s, c_r,
    q_s, q_r, qm_s, qm_r, m_s, m_r, r_s, r_r, g_s, g_r, w_s, w_r,
    a_s, a_r, x_s, x_r, p_s, p_r, s_s, s_r, o_s, o_r, z_s, z_r, f_s, f_r,
):
    c = lax.axis_index("ctx")
    t = lax.axis_index("tp")
    z = lax.rem(c, 16)
    yh = c // 16
    core = lax.rem(t, 2)
    group = t // 2
    par = lax.rem(z, 2)
    mate_z = z + 1 - 2 * par
    pair = z // 2
    zr = lax.rem(z, 4)
    zq = z // 4
    partner = ((1 - yh) * 16 + z, t)
    other_core = (c, t + 1 - 2 * core)
    sends = []

    def zdev(d):
        return (yh * 16 + lax.rem(z + 16 + d, 16), t)

    def tdev(d):
        return (c, lax.rem(t + d, 16))

    def send(src, dst, ssem, rsem, dev):
        copy = pltpu.make_async_remote_copy(
            src_ref=src, dst_ref=dst, send_sem=ssem, recv_sem=rsem, device_id=dev, device_id_type=MESH
        )
        copy.start()
        sends.append(copy)

    def elsewhere(dev):
        return jnp.logical_not((dev[0] == c) & (dev[1] == t))

    def either(src, dst, ssem, rsem, dev):
        @pl.when(elsewhere(dev))
        def _():
            pltpu.make_async_remote_copy(
                src_ref=src, dst_ref=dst, send_sem=ssem, recv_sem=rsem, device_id=dev, device_id_type=MESH
            ).start()

        @pl.when(jnp.logical_not(elsewhere(dev)))
        def _():
            pltpu.make_async_copy(src, dst, rsem).start()

    def either_sent(src, ssem, dev):
        @pl.when(elsewhere(dev))
        def _():
            arrived(src, ssem)

    def arrived(dst, rsem):
        pltpu.make_async_copy(dst, dst, rsem).wait()

    barrier = pltpu.get_barrier_semaphore()

    def greet(dev):
        pl.semaphore_signal(barrier, inc=1, device_id=dev, device_id_type=MESH)

    for d in range(1, 16):
        greet(zdev(d))
        greet(tdev(d))
    greet(partner)
    greet(((1 - yh) * 16 + mate_z, t))
    half_t, slot_t = t // 8, lax.rem(t, 8)
    res_mid = (c, lax.rem(yh + half_t, 2) * 8 + lax.rem(slot_t + 64 - 3 * pair, 8))
    held_pair = lax.rem(slot_t + 3 * pair, 8)
    held_half = lax.rem(half_t + yh, 2)
    res_pair = lax.rem(3 * (pair + 8 - slot_t), 8)

    def res_dest(g):
        return ((g // 2) * 16 + 2 * held_pair + g % 2, t)

    def res_source(j):
        return lax.rem(half_t + j, 2)

    res_peers = [res_dest(g) for g in range(4)] + [
        (res_source(j) * 16 + 2 * res_pair + p, t) for j in range(2) for p in range(2)
    ]
    n_peers = 32
    for dev in res_peers:
        n_peers += jnp.where(elsewhere(dev), 1, 0)

        @pl.when(elsewhere(dev))
        def _(dev=dev):
            greet(dev)

    w_here = yh * 2 + par
    wo_rows = pl.ds(pl.multiple_of(w_here * 160, 16), 160)
    lanes = pl.ds(pl.multiple_of(group * HD, HD), HD)
    here = kv.at[core, yh, zr, zq]
    fetches = [
        pltpu.make_async_copy(pos_hbm, pos_ref, in_s.at[0]),
        pltpu.make_async_copy(q_hbm.at[:, pl.ds(0, HD)], qall.at[pl.ds(0, TOK)], in_s.at[1]),
        pltpu.make_async_copy(q_hbm.at[:, pl.ds(HD, HD)], qall.at[pl.ds(160, TOK)], in_s.at[2]),
        pltpu.make_async_copy(res_hbm, res_ref, in_s.at[3]),
        pltpu.make_async_copy(gain_hbm, gain_ref, in_s.at[4]),
        pltpu.make_async_copy(lw_hbm, lw_ref, in_s.at[5]),
        pltpu.make_async_copy(wo_hbm, wob.at[wo_rows], in_s.at[6]),
        pltpu.make_async_copy(wm_hbm, wmb.at[wo_rows], in_s.at[7]),
    ]

    @pl.when(core == 0)
    def _():
        pltpu.make_async_copy(k_hbm.at[:, lanes], here, in_s.at[8]).start()

    @pl.when(core == 1)
    def _():
        pltpu.make_async_copy(v_hbm.at[:, lanes], here, in_s.at[8]).start()

    for fetch in fetches:
        fetch.start()

    fetches[0].wait()
    pos8 = pos_ref[...]
    hi8 = (pos8 >> 6).astype(F32).astype(BF16)
    lo8 = (pos8 & 63).astype(F32).astype(BF16)
    eye128 = shift(128, 128, 0)
    post = (nt(eye128, hi8) * 64.0 + nt(eye128, lo8)).astype(I32)
    base = c * TOK

    def before(limit):
        hits = jnp.where(pos8 < limit, 1.0, 0.0)
        return jnp.sum(jnp.sum(hits, axis=1, keepdims=True), axis=0, keepdims=True).astype(I32)

    first = before(base)
    selq = jnp.zeros((256, TOK), F32)
    lane_q = iota((128, 256), 1)
    owner_q = ((lane_q >> 3) & 1) * 16 + (lane_q >> 4)

    def held_steps(a):
        col = post[:, a : a + 1]
        step = iota((128, 1), 0) + a * 128
        rank = jnp.where((col >= base) & (col < base + TOK), (step - first) >> 5, 1000)
        return step & 31, rank, (col == iota((128, TOK), 1) + base).astype(BF16)

    for a in range(8):
        owner, rank, held = held_steps(a)
        selq += tn(((owner == owner_q) & (rank == (lane_q & 3))).astype(BF16), held)
    selq = selq.astype(BF16)
    head_row = (iota((256, 128), 0) >> 2) & 1
    fetches[1].wait()
    fetches[2].wait()
    qsend[...] = jnp.where(
        head_row == 0, nn(selq, qall[0:TOK]), nn(selq, qall[160 : 160 + TOK])
    ).astype(BF16)

    def rows_of(count, owner):
        pick = ((iota((count, 8), 0) & 31) >> 2 == iota((count, 8), 1)).astype(BF16)
        spread = nn(pick, hi8) * 64.0 + nn(pick, lo8)
        lane = (iota((count, 128), 0) & 3) * 32 + owner
        return jnp.sum(jnp.where(iota((count, 128), 1) == lane, spread, 0.0), axis=1, keepdims=True)

    pl.semaphore_wait(barrier, n_peers)

    arrived(here, in_s.at[8])

    def kv_block(plane, n, f):
        py = yh if plane == 0 else 1 - yh
        from_z = lax.rem(z + (0, 15, 1, 14)[n] + 16 - 4 * f, 16)
        return kv.at[core, py, lax.rem(from_z, 4), from_z // 4]

    def kv_bundle(plane, n, kind):
        py = yh if plane == 0 else 1 - yh
        return kv.at[kind, py, lax.rem(zr + (0, 3, 1, 2)[n], 4)]

    def kv_pass(plane, f):
        block = kv_block(plane, 0, f)
        if plane == 0:
            if f in (0, 1):
                send(block, block, near_s.at[0, 3, f], near_r.at[0, 3, f], zdev(2))
            if f in (0, 3):
                send(block, block, near_s.at[0, 3, 2 + f // 3], near_r.at[0, 3, 2 + f // 3], zdev(-2))
        for n, d in ((1, 1), (2, -1)):
            send(block, block, near_s.at[plane, n, f], near_r.at[plane, n, f], zdev(d))

    def kv_cross(n, f):
        block = kv_block(0, n, f)
        send(block, block, y_s.at[n // 3, f], y_r.at[n // 3, f], partner)

    def kv_core(plane, n):
        bundle = kv_bundle(plane, n, core)
        send(bundle, bundle, c_s.at[plane, n], c_r.at[plane, n], other_core)

    def weight_rows(r):
        slot = (yh if r < 2 else 1 - yh) * 2 + (par if r % 2 == 0 else 1 - par)
        return pl.ds(pl.multiple_of(slot * 160, 16), 160)

    def weight_send(w, r):
        buffer = (wob, wmb)[w]
        rows = weight_rows(1) if r == 3 else wo_rows
        dev = (yh * 16 + mate_z, t) if r == 1 else partner
        send(buffer.at[rows], buffer.at[rows], w_s.at[w, r], w_r.at[w, r], dev)

    def weight_wait(w, r):
        arrived((wob, wmb)[w].at[weight_rows(r)], w_r.at[w, r])

    for f in (2, 1, 3):
        send(here, here, far_s.at[f], far_r.at[f], zdev(4 * f))
    kv_cross(0, 0)
    for d in (8, 7, 9, 6, 10, 5, 11, 4, 12, 3, 13, 2, 14, 1, 15):
        zd = lax.rem(z + d, 16)
        send(
            qsend.at[pl.ds(zd * 16, 16)], qrecv.at[pl.ds(z * 16, 16)], q_s.at[d], q_r.at[d], zdev(d)
        )
    qrecv[pl.ds(pl.multiple_of(z * 16, 16), 16)] = qsend[pl.ds(pl.multiple_of(z * 16, 16), 16)]
    kv_pass(0, 0)
    fetches[6].wait()
    weight_send(0, 2)
    weight_send(0, 1)
    mine = rows_of(STEPS, c)
    for h in range(2):
        posc[h * 160 : h * 160 + TOK] = iota((TOK, 128), 0) + base
        posc[h * 160 + TOK : (h + 1) * 160] = jnp.broadcast_to(mine.astype(I32), (STEPS, 128))
    selr = jnp.zeros((128, TOK), F32)
    lane_r = iota((128, 128), 1)
    owner_r = (lane_r >> 6) * 16 + ((lane_r >> 2) & 7) * 2 + ((lane_r >> 5) & 1)
    for a in range(8):
        owner, rank, held = held_steps(a)
        selr += tn(((owner == owner_r) & (rank == (lane_r & 3))).astype(BF16), held)
    fetches[3].wait()
    rsend[...] = nt(selr.astype(BF16), res_ref[...]).astype(BF16)
    fetches[4].wait()
    either(rsend, rmid, m_s, m_r, res_mid)
    gbuf[t] = jnp.broadcast_to(gain_ref[...].astype(F32).reshape(1, 320), (16, 320)).astype(BF16)
    for d in range(1, 16):
        send(gbuf.at[t], gbuf.at[t], g_s.at[d], g_r.at[d], tdev(d))
    fetches[5].wait()
    lwt[...] = nn(nt(eye128, lw_ref[...]).astype(BF16), shift(320, 384, 0)).astype(BF16)

    arrived(kv_block(1, 0, 0), y_r.at[0, 0])
    kv_pass(1, 0)

    def kv_far(f):
        arrived(kv_block(0, 0, f), far_r.at[f])
        kv_cross(0, f)
        kv_pass(0, f)

    def kv_two(i, f):
        arrived(kv_block(0, 3, f), near_r.at[0, 3, i])
        kv_cross(3, f)

    def kv_other(f):
        arrived(kv_block(1, 0, f), y_r.at[0, f])
        kv_pass(1, f)

    kv_far(1)
    kv_far(3)
    kv_two(0, 0)
    kv_two(2, 3)
    kv_far(2)
    kv_core(0, 0)
    weight_wait(0, 1)
    weight_send(0, 3)

    for d in range(1, 16):
        from_z = lax.rem(z + 16 - d, 16)
        arrived(qrecv.at[pl.ds(from_z * 16, 16)], q_r.at[d])
    lane = iota((STEPS, 256), 1)
    for which in range(2):
        o_y = yh if which == 0 else 1 - yh
        spots = rows_of(STEPS, o_y * 16 + z).astype(I32)
        source = spots >> 7
        diagonal = iota((STEPS, STEPS), 0) == iota((STEPS, STEPS), 1)
        source_row = jnp.sum(
            jnp.where(diagonal, source.astype(F32), 0.0), axis=0, keepdims=True
        ).astype(I32)
        earlier = iota((STEPS, STEPS), 1) < iota((STEPS, STEPS), 0)
        rank = jnp.sum(
            jnp.where((source == source_row) & earlier, 1.0, 0.0), axis=1, keepdims=True
        ).astype(I32)
        for h in range(2):
            wanted = (source & 15) * 16 + o_y * 8 + h * 4 + rank
            take = ((wanted == lane) & (source >> 4 == yh)).astype(BF16)
            rows = nn(take, qrecv[...]).astype(BF16)
            if which == 0:
                qall[h * 160 + TOK : (h + 1) * 160] = rows
            else:
                qmid_s[h * STEPS : (h + 1) * STEPS] = rows
    send(qmid_s, qmid_r, qm_s, qm_r, partner)

    state = [jnp.full((320, 1), MASKED, F32), jnp.zeros((320, 1), F32), jnp.zeros((320, HD), F32)]

    def attend(p, n):
        py = yh if p == 0 else 1 - yh
        set_ = lax.rem(zr + (0, 3, 1, 2)[n], 4)
        arrived(kv_bundle(p, n, 1 - core), c_r.at[p, n])
        keys = kv[0, py, set_].reshape(512, HD)
        values = kv[1, py, set_].reshape(512, HD)
        highest, totals, accum = state
        scores = nt(qall[...], keys) * (HD**-0.5)
        kk = iota((320, 512), 1)
        spot = (py * 16 + set_) * TOK + (kk >> 7) * 512 + (kk & 127)
        scores = jnp.where(spot <= posc[:, 0:1], scores, MASKED)
        new = jnp.maximum(highest, jnp.max(scores, axis=1, keepdims=True))
        alpha = jnp.exp(highest - new)
        weights = jnp.exp(scores - new)
        state[0] = new
        state[1] = totals * alpha + jnp.sum(weights, axis=1, keepdims=True)
        state[2] = accum * alpha + nn(weights.astype(BF16), values)

    kv_other(1)
    kv_other(3)
    kv_two(1, 1)
    kv_two(3, 2)
    kv_core(0, 3)
    kv_other(2)
    kv_core(1, 0)
    arrived(qmid_r, qm_r)
    for h in range(2):
        rows = slice(h * 160 + TOK, (h + 1) * 160)
        qall[rows] = (
            qall[rows].astype(F32) + qmid_r[h * STEPS : (h + 1) * STEPS].astype(F32)
        ).astype(BF16)
    arrived(rmid, m_r)
    for g in range(4):
        either(rmid.at[pl.ds(g * 32, 32)], rbuf.at[held_half, par], r_s.at[g], r_r.at[held_half, par], res_dest(g))

    attend(0, 0)
    for n in (1, 2):
        for f in range(4):
            arrived(kv_block(0, n, f), near_r.at[0, n, f])
        kv_core(0, n)
    attend(1, 0)
    attend(0, 3)
    for n in (1, 2):
        for f in range(4):
            arrived(kv_block(1, n, f), near_r.at[1, n, f])
        kv_core(1, n)

    for bundle in ((0, 1), (0, 2), (1, 1)):
        attend(*bundle)
    for f in range(4):
        arrived(kv_block(1, 3, f), y_r.at[1, f])
    kv_core(1, 3)
    attend(1, 2)
    attend(1, 3)
    mixed = (state[2] / state[1]).astype(BF16)
    k_rows = pl.ds(pl.multiple_of(pair * STEPS, STEPS), STEPS)
    for h in range(2):
        agrp[k_rows, h * HD : (h + 1) * HD] = mixed[h * 160 + TOK : (h + 1) * 160]

    for d in (4, 3, 5, 2, 6, 1, 7):
        send(agrp.at[k_rows], agrp.at[k_rows], a_s.at[d], a_r.at[d], zdev(2 * d))
    for h in range(2):
        att_ref[:, h * HD : (h + 1) * HD] = mixed[h * 160 : h * 160 + TOK]

    for d in range(1, 16):
        src_t = lax.rem(t + 16 - d, 16)
        arrived(gbuf.at[src_t], g_r.at[d])
    gain = nn(gbuf[pair], shift(320, COLS, 0)) + nn(gbuf[8 + pair], shift(320, COLS, 320))
    gain = gain[0:1]
    for j in range(2):
        for s in range(2):
            arrived(rbuf.at[j, s], r_r.at[j, s])
    row = iota((256, 1), 0)
    spots = rows_of(256, yh * 16 + 2 * (iota((256, 128), 0) >> 5) + par).astype(I32)
    step = (row & 31) * 32 + yh * 16 + 2 * (row >> 5) + par
    slot = iota((256, 64), 1)
    res_part = jnp.zeros((256, COLS), F32)
    for j in range(2):
        source = res_source(j) * 16 + 2 * res_pair
        nth = (spots >> 7) - source
        rank = (step - jnp.where(nth == 0, before(source * TOK), before((source + 1) * TOK))) >> 5
        wanted = jnp.where((nth == 0) | (nth == 1), nth * 32 + (row >> 5) * 4 + rank, 1000)
        rows = nn((wanted == slot).astype(BF16), rbuf[j].reshape(64, 320)).astype(BF16)
        res_part += nn(rows, shift(320, COLS, j * 320))

    res_add[...] = res_part

    weight_wait(0, 2)
    weight_wait(0, 3)
    for d in range(1, 8):
        from_k = lax.rem(pair + 8 - d, 8)
        arrived(agrp.at[pl.ds(pl.multiple_of(from_k * STEPS, STEPS), STEPS)], a_r.at[d])
    mine = pl.ds(pl.multiple_of(core * 128, 128), 128)
    theirs = pl.ds(pl.multiple_of((1 - core) * 128, 128), 128)
    chip = t // 2
    pb[...] = (nt(agrp[theirs], wob[...]) + res_add[theirs]).astype(BF16)
    send(pb, px, x_s.at[0], x_r.at[0], other_core)
    partial = nt(agrp[mine], wob[...]) + res_add[mine]
    arrived(px, x_r.at[0])
    ph[...] = (partial + px[...].astype(F32)).astype(BF16)

    def chip_rows(index):
        return pl.ds(pl.multiple_of(index * 16, 16), 16)

    for d in (4, 3, 5, 2, 6, 1, 7):
        send(ph.at[chip_rows(lax.rem(chip + d, 8))], rb.at[chip], p_s.at[d], p_r.at[d], tdev(2 * d))
    fetches[7].wait()
    weight_send(1, 1)
    weight_send(1, 2)
    total = ph[chip_rows(chip)].astype(F32)
    for d in range(1, 8):
        src = lax.rem(chip + 8 - d, 8)
        arrived(rb.at[src], p_r.at[d])
        total += rb[src].astype(F32)
    own_rows = chip_rows(core * 8 + chip)
    sb[own_rows] = total.astype(BF16)
    for d in (4, 3, 5, 2, 6, 1, 7):
        send(sb.at[own_rows], sb.at[own_rows], s_s.at[d], s_r.at[d], tdev(2 * d))
    weight_wait(1, 1)
    weight_send(1, 3)
    weight_wait(1, 2)
    for d in range(1, 8):
        arrived(sb.at[chip_rows(core * 8 + lax.rem(chip + 8 - d, 8))], s_r.at[d])
    send(sb.at[mine], sb.at[mine], x_s.at[1], x_r.at[1], other_core)
    weight_wait(1, 3)
    wmbig[...] = nn(wmb[...], shift(320, 384, 0)).astype(BF16)

    def score(rows, first_owner):
        states = sb[rows].astype(F32)
        squares = jnp.sum(states * states, axis=1, keepdims=True)
        pre = nn((states * gain).astype(BF16), wmbig[...])
        sq_hi = squares.astype(BF16).astype(F32)
        col = iota((128, 384), 1)
        pre = jnp.where(col == 320, sq_hi, jnp.where(col == 321, squares - sq_hi, pre))
        yb[rows] = pre.astype(BF16)
        for m in range(4):
            k = first_owner + m
            piece = yb.at[pl.ds(pl.multiple_of(k * STEPS, STEPS), STEPS)]

            @pl.when(k != pair)
            def _(k=k, piece=piece):
                pltpu.make_async_remote_copy(
                    src_ref=piece, dst_ref=yr.at[pair], send_sem=z_s.at[k], recv_sem=z_r.at[pair],
                    device_id=(yh * 16 + 2 * k + par, t), device_id_type=MESH,
                ).start()

    score(mine, core * 4)
    arrived(sb.at[theirs], x_r.at[1])
    score(theirs, (1 - core) * 4)

    out_k = lax.rem(slot_t + 3 * pair, 8)
    block = sb[pl.ds(pl.multiple_of(out_k * STEPS, STEPS), STEPS)]
    ob_s[...] = nn(
        block, (iota((COLS, 320), 0) == iota((COLS, 320), 1) + half_t * 320).astype(BF16)
    ).astype(BF16)

    out_z = (yh * 16 + 2 * out_k + par, t)
    out_t = (c, half_t * 8 + lax.rem(3 * (pair + 8 - slot_t), 8))
    either(ob_s, ob_z, o_s.at[0], o_r.at[0], out_z)

    yr[pair] = yb[k_rows]
    for k in range(8):

        @pl.when(k != pair)
        def _(k=k):
            arrived(yr.at[k], z_r.at[k])

    total = yr[0].astype(F32)
    for k in range(1, 8):
        total += yr[k].astype(F32)
    col = iota((STEPS, 384), 1)
    squares = jnp.sum(jnp.where((col == 320) | (col == 321), total, 0.0), axis=1, keepdims=True)
    pre = jnp.where(col < 320, total * lax.rsqrt(squares / D + 1e-06), 0.0)
    arrived(ob_z, o_r.at[0])
    either(ob_z, ob, o_s.at[1], o_r.at[1], out_t)
    hidden = (pre / (1.0 + jnp.exp(-pre))).astype(BF16)
    fb[...] = nt(lwt[...], hidden)
    for d in range(1, 16):
        to_t = lax.rem(t + d, 16)
        send(fb.at[pl.ds(pl.multiple_of(to_t * 8, 8), 8)], fr.at[t], f_s.at[d], f_r.at[d], tdev(d))
    arrived(ob, o_r.at[1])
    states_ref[...] = ob[...]
    total = fb[pl.ds(pl.multiple_of(t * 8, 8), 8)]
    for d in range(1, 16):
        src_t = lax.rem(t + 16 - d, 16)
        arrived(fr.at[src_t], f_r.at[d])
        total += fr[src_t]
    levels_ref[...] = total

    for copy in sends:
        copy.wait_send()
    either_sent(rsend, m_s, res_mid)
    for g in range(4):
        either_sent(rmid.at[pl.ds(g * 32, 32)], r_s.at[g], res_dest(g))

    for k in range(8):

        @pl.when(k != pair)
        def _(k=k):
            arrived(yr.at[k], z_s.at[k])

    either_sent(ob_s, o_s.at[0], out_z)
    either_sent(ob_z, o_s.at[1], out_t)


def on_device(q, k, v, res, wo, gain, wm, lw, positions):
    vmem = pl.BlockSpec(memory_space=pltpu.VMEM)
    dma = pltpu.SemaphoreType.DMA
    scratch = [
        pltpu.VMEM((320, TOK), BF16),
        pltpu.VMEM((320,), BF16),
        pltpu.VMEM((320, 128), BF16),
        pltpu.VMEM((8, 128), I32),
        pltpu.VMEM((2, 2, 4, 4, TOK, HD), BF16),
        pltpu.VMEM((320, HD), BF16),
        pltpu.VMEM((256, HD), BF16),
        pltpu.VMEM((256, HD), BF16),
        pltpu.VMEM((64, HD), BF16),
        pltpu.VMEM((64, HD), BF16),
        pltpu.VMEM((320, 128), I32),
        pltpu.VMEM((128, 320), BF16),
        pltpu.VMEM((128, 320), BF16),
        pltpu.VMEM((2, 2, 32, 320), BF16),
        pltpu.VMEM((16, 16, 320), BF16),
        pltpu.VMEM((COLS, 256), BF16),
        pltpu.VMEM((COLS, 320), BF16),
        pltpu.VMEM((COLS, 384), BF16),
        pltpu.VMEM((128, 384), BF16),
        pltpu.VMEM((256, 256), BF16),
        pltpu.VMEM((256, COLS), F32),
        pltpu.VMEM((128, COLS), BF16),
        pltpu.VMEM((128, COLS), BF16),
        pltpu.VMEM((128, COLS), BF16),
        pltpu.VMEM((8, 16, COLS), BF16),
        pltpu.VMEM((256, COLS), BF16),
        pltpu.VMEM((32, 320), BF16),
        pltpu.VMEM((32, 320), BF16),
        pltpu.VMEM((32, 320), BF16),
        pltpu.VMEM((256, 384), BF16),
        pltpu.VMEM((8, 32, 384), BF16),
        pltpu.VMEM((128, 32), F32),
        pltpu.VMEM((16, 8, 32), F32),
        dma((9,)), dma((4,)), dma((4,)), dma((2, 4, 4)), dma((2, 4, 4)), dma((2, 4)), dma((2, 4)), dma((2, 4)), dma((2, 4)),
        dma((16,)), dma((16,)), dma(()), dma(()), dma(()), dma(()), dma((4,)), dma((2, 2)), dma((16,)), dma((16,)), dma((2, 4)), dma((2, 4)),
        dma((8,)), dma((8,)), dma((2,)), dma((2,)), dma((8,)), dma((8,)), dma((8,)), dma((8,)), dma((2,)), dma((2,)), dma((8,)), dma((8,)), dma((16,)), dma((16,)),
    ]
    attended, states, levels = pl.pallas_call(
        kernel,
        out_shape=(
            jax.ShapeDtypeStruct((TOK, 2 * HD), BF16),
            jax.ShapeDtypeStruct((STEPS, 320), BF16),
            jax.ShapeDtypeStruct((8, STEPS), F32),
        ),
        in_specs=[pl.BlockSpec(memory_space=pltpu.HBM)] * 9,
        out_specs=(vmem, vmem, vmem),
        scratch_shapes=scratch,
        compiler_params=pltpu.CompilerParams(
            collective_id=0, has_side_effects=True, vmem_limit_bytes=56 * 1024 * 1024
        ),
    )(q, k, v, res.T, wo.T, gain, wm, lw, positions.reshape(8, 128))
    return attended, states, levels.T


def solution(mesh):
    in_specs = (
        P("ctx", "tp"),
        P("ctx", None),
        P("ctx", None),
        P("ctx", "tp"),
        P("tp", "ctx"),
        P("tp"),
        P("ctx", "tp"),
        P("tp", None),
        P(),
    )
    out_specs = (P("ctx", "tp"), P("ctx", "tp"), P("ctx", "tp"))
    return jax.shard_map(
        on_device, mesh=mesh, in_specs=in_specs, out_specs=out_specs, check_vma=False
    )
```

```python
import functools

import jax
import jax.numpy as jnp
from jax import lax
from jax.experimental import pallas as pl
from jax.experimental.pallas import tpu as pltpu
from jax.sharding import PartitionSpec as P

D = 5120
HD = 128
TOK = 128
STEPS = 32
COLS = 640
MASKED = -1e30
MESH = pl.DeviceIdType.MESH
F32 = jnp.float32
BF16 = jnp.bfloat16
I32 = jnp.int32


def iota(shape, dim):
    return lax.broadcasted_iota(I32, shape, dim)


def nn(a, b):
    return lax.dot_general(a, b, (((1,), (0,)), ((), ())), preferred_element_type=F32)


def nt(a, b):
    return lax.dot_general(a, b, (((1,), (1,)), ((), ())), preferred_element_type=F32)


def tn(a, b):
    return lax.dot_general(a, b, (((0,), (0,)), ((), ())), preferred_element_type=F32)


def shift(rows, cols, offset):
    return (iota((rows, cols), 0) + offset == iota((rows, cols), 1)).astype(BF16)


def kernel(
    q_hbm, k_hbm, v_hbm, res_hbm, wo_hbm, gain_hbm, wm_hbm, lw_hbm, pos_hbm,
    att_ref, states_ref, levels_ref,
    res_ref, gain_ref, lw_ref, pos_ref, kv, qall, qsend, qrecv, qmid_s, qmid_r, posc,
    rsend, rmid, rbuf, gbuf, wob, wmb, wmbig, lwt,
    agrp, res_add, pb, px, ph, rb, sb, ob_s, ob_z, ob, yb, yr, fb, fr,
    in_s, far_s, far_r, near_s, near_r, y_s, y_r, c_s, c_r,
    q_s, q_r, qm_s, qm_r, m_s, m_r, r_s, r_r, g_s, g_r, w_s, w_r,
    a_s, a_r, x_s, x_r, p_s, p_r, s_s, s_r, o_s, o_r, z_s, z_r, f_s, f_r,
):
    c = lax.axis_index("ctx")
    t = lax.axis_index("tp")
    z = lax.rem(c, 16)
    yh = c // 16
    core = lax.rem(t, 2)
    group = t // 2
    par = lax.rem(z, 2)
    mate_z = z + 1 - 2 * par
    pair = z // 2
    zr = lax.rem(z, 4)
    zq = z // 4
    partner = ((1 - yh) * 16 + z, t)
    other_core = (c, t + 1 - 2 * core)
    sends = []

    def zdev(d):
        return (yh * 16 + lax.rem(z + 16 + d, 16), t)

    def tdev(d):
        return (c, lax.rem(t + d, 16))

    def send(src, dst, ssem, rsem, dev):
        copy = pltpu.make_async_remote_copy(
            src_ref=src, dst_ref=dst, send_sem=ssem, recv_sem=rsem, device_id=dev, device_id_type=MESH
        )
        copy.start()
        sends.append(copy)

    def elsewhere(dev):
        return jnp.logical_not((dev[0] == c) & (dev[1] == t))

    def either(src, dst, ssem, rsem, dev):
        @pl.when(elsewhere(dev))
        def _():
            pltpu.make_async_remote_copy(
                src_ref=src, dst_ref=dst, send_sem=ssem, recv_sem=rsem, device_id=dev, device_id_type=MESH
            ).start()

        @pl.when(jnp.logical_not(elsewhere(dev)))
        def _():
            pltpu.make_async_copy(src, dst, rsem).start()

    def either_sent(src, ssem, dev):
        @pl.when(elsewhere(dev))
        def _():
            arrived(src, ssem)

    def arrived(dst, rsem):
        pltpu.make_async_copy(dst, dst, rsem).wait()

    barrier = pltpu.get_barrier_semaphore()

    def greet(dev):
        pl.semaphore_signal(barrier, inc=1, device_id=dev, device_id_type=MESH)

    for d in range(1, 16):
        greet(zdev(d))
        greet(tdev(d))
    greet(partner)
    greet(((1 - yh) * 16 + mate_z, t))
    half_t, slot_t = t // 8, lax.rem(t, 8)
    res_mid = (c, lax.rem(yh + half_t, 2) * 8 + lax.rem(slot_t + 64 - 3 * pair, 8))
    held_pair = lax.rem(slot_t + 3 * pair, 8)
    held_half = lax.rem(half_t + yh, 2)
    res_pair = lax.rem(3 * (pair + 8 - slot_t), 8)

    def res_dest(g):
        return ((g // 2) * 16 + 2 * held_pair + g % 2, t)

    def res_source(j):
        return lax.rem(half_t + j, 2)

    res_peers = [res_dest(g) for g in range(4)] + [
        (res_source(j) * 16 + 2 * res_pair + p, t) for j in range(2) for p in range(2)
    ]
    n_peers = 32
    for dev in res_peers:
        n_peers += jnp.where(elsewhere(dev), 1, 0)

        @pl.when(elsewhere(dev))
        def _(dev=dev):
            greet(dev)

    w_here = yh * 2 + par
    wo_rows = pl.ds(pl.multiple_of(w_here * 160, 16), 160)
    lanes = pl.ds(pl.multiple_of(group * HD, HD), HD)
    here = kv.at[core, yh, zr, zq]
    fetches = [
        pltpu.make_async_copy(pos_hbm, pos_ref, in_s.at[0]),
        pltpu.make_async_copy(q_hbm.at[:, pl.ds(0, HD)], qall.at[pl.ds(0, TOK)], in_s.at[1]),
        pltpu.make_async_copy(q_hbm.at[:, pl.ds(HD, HD)], qall.at[pl.ds(160, TOK)], in_s.at[2]),
        pltpu.make_async_copy(res_hbm, res_ref, in_s.at[3]),
        pltpu.make_async_copy(gain_hbm, gain_ref, in_s.at[4]),
        pltpu.make_async_copy(lw_hbm, lw_ref, in_s.at[5]),
        pltpu.make_async_copy(wo_hbm, wob.at[wo_rows], in_s.at[6]),
        pltpu.make_async_copy(wm_hbm, wmb.at[wo_rows], in_s.at[7]),
    ]

    @pl.when(core == 0)
    def _():
        pltpu.make_async_copy(k_hbm.at[:, lanes], here, in_s.at[8]).start()

    @pl.when(core == 1)
    def _():
        pltpu.make_async_copy(v_hbm.at[:, lanes], here, in_s.at[8]).start()

    for fetch in fetches:
        fetch.start()

    fetches[0].wait()
    pos8 = pos_ref[...]
    hi8 = (pos8 >> 6).astype(F32).astype(BF16)
    lo8 = (pos8 & 63).astype(F32).astype(BF16)
    eye128 = shift(128, 128, 0)
    base = c * TOK

    def before(limit):
        hits = jnp.where(pos8 < limit, 1.0, 0.0)
        return jnp.sum(jnp.sum(hits, axis=1, keepdims=True), axis=0, keepdims=True).astype(I32)

    first = before(base)
    selq = jnp.zeros((256, TOK), F32)
    slot_q = iota((256, 128), 0)
    key_q = (((slot_q >> 3) & 1) * 16 + (slot_q >> 4)) * 4 + (slot_q & 3)

    def held_steps(a):
        spot = pos8[a : a + 1]
        step = iota((1, 128), 1) + a * 128
        here_too = (spot >= base) & (spot < base + TOK)
        key = jnp.where(here_too, (step & 31) * 4 + ((step - first) >> 5), -1)
        return key, (spot == iota((TOK, 128), 0) + base).astype(BF16)

    for a in range(8):
        key, held = held_steps(a)
        selq += nt((key == key_q).astype(BF16), held)
    selq = selq.astype(BF16)
    head_row = (iota((256, 128), 0) >> 2) & 1
    fetches[1].wait()
    fetches[2].wait()
    qsend[...] = jnp.where(
        head_row == 0, nn(selq, qall[0:TOK]), nn(selq, qall[160 : 160 + TOK])
    ).astype(BF16)

    def rows_of(count, owner):
        pick = ((iota((count, 8), 0) & 31) >> 2 == iota((count, 8), 1)).astype(BF16)
        spread = nn(pick, hi8) * 64.0 + nn(pick, lo8)
        lane = (iota((count, 128), 0) & 3) * 32 + owner
        return jnp.sum(jnp.where(iota((count, 128), 1) == lane, spread, 0.0), axis=1, keepdims=True)

    pl.semaphore_wait(barrier, n_peers)

    arrived(here, in_s.at[8])

    def kv_block(plane, n, f):
        py = yh if plane == 0 else 1 - yh
        from_z = lax.rem(z + (0, 15, 1, 14)[n] + 16 - 4 * f, 16)
        return kv.at[core, py, lax.rem(from_z, 4), from_z // 4]

    def kv_bundle(plane, n, kind):
        py = yh if plane == 0 else 1 - yh
        return kv.at[kind, py, lax.rem(zr + (0, 3, 1, 2)[n], 4)]

    def kv_pass(plane, f):
        block = kv_block(plane, 0, f)
        if plane == 0:
            if f in (0, 1):
                send(block, block, near_s.at[0, 3, f], near_r.at[0, 3, f], zdev(2))
            if f in (0, 3):
                send(block, block, near_s.at[0, 3, 2 + f // 3], near_r.at[0, 3, 2 + f // 3], zdev(-2))
        for n, d in ((1, 1), (2, -1)):
            send(block, block, near_s.at[plane, n, f], near_r.at[plane, n, f], zdev(d))

    def kv_cross(n, f):
        block = kv_block(0, n, f)
        send(block, block, y_s.at[n // 3, f], y_r.at[n // 3, f], partner)

    def kv_core(plane, n):
        bundle = kv_bundle(plane, n, core)
        send(bundle, bundle, c_s.at[plane, n], c_r.at[plane, n], other_core)

    def weight_rows(r):
        slot = (yh if r < 2 else 1 - yh) * 2 + (par if r % 2 == 0 else 1 - par)
        return pl.ds(pl.multiple_of(slot * 160, 16), 160)

    def weight_send(w, r):
        buffer = (wob, wmb)[w]
        rows = weight_rows(1) if r == 3 else wo_rows
        dev = (yh * 16 + mate_z, t) if r == 1 else partner
        send(buffer.at[rows], buffer.at[rows], w_s.at[w, r], w_r.at[w, r], dev)

    def weight_wait(w, r):
        arrived((wob, wmb)[w].at[weight_rows(r)], w_r.at[w, r])

    for f in (2, 1, 3):
        send(here, here, far_s.at[f], far_r.at[f], zdev(4 * f))
    kv_cross(0, 0)
    for d in (8, 7, 9, 6, 10, 5, 11, 4, 12, 3, 13, 2, 14, 1, 15):
        zd = lax.rem(z + d, 16)
        send(
            qsend.at[pl.ds(zd * 16, 16)], qrecv.at[pl.ds(z * 16, 16)], q_s.at[d], q_r.at[d], zdev(d)
        )
    qrecv[pl.ds(pl.multiple_of(z * 16, 16), 16)] = qsend[pl.ds(pl.multiple_of(z * 16, 16), 16)]
    kv_pass(0, 0)
    fetches[6].wait()
    weight_send(0, 2)
    fetches[7].wait()
    weight_send(1, 2)
    weight_send(0, 1)
    mine = rows_of(STEPS, c)
    for h in range(2):
        posc[h * 160 : h * 160 + TOK] = iota((TOK, 128), 0) + base
        posc[h * 160 + TOK : (h + 1) * 160] = jnp.broadcast_to(mine.astype(I32), (STEPS, 128))
    selr = jnp.zeros((128, TOK), F32)
    slot_r = iota((128, 128), 0)
    key_r = ((slot_r >> 6) * 16 + ((slot_r >> 2) & 7) * 2 + ((slot_r >> 5) & 1)) * 4 + (slot_r & 3)
    for a in range(8):
        key, held = held_steps(a)
        selr += nt((key == key_r).astype(BF16), held)
    fetches[3].wait()
    rsend[...] = nt(selr.astype(BF16), res_ref[...]).astype(BF16)
    fetches[4].wait()
    either(rsend, rmid, m_s, m_r, res_mid)
    gbuf[t] = jnp.broadcast_to(gain_ref[...].astype(F32).reshape(1, 320), (16, 320)).astype(BF16)
    for d in range(1, 16):
        send(gbuf.at[t], gbuf.at[t], g_s.at[d], g_r.at[d], tdev(d))
    fetches[5].wait()
    lwt[...] = nn(nt(eye128, lw_ref[...]).astype(BF16), shift(320, 384, 0)).astype(BF16)

    arrived(kv_block(1, 0, 0), y_r.at[0, 0])
    kv_pass(1, 0)

    def kv_far(f):
        arrived(kv_block(0, 0, f), far_r.at[f])
        kv_cross(0, f)
        kv_pass(0, f)

    def kv_two(i, f):
        arrived(kv_block(0, 3, f), near_r.at[0, 3, i])
        kv_cross(3, f)

    def kv_other(f):
        arrived(kv_block(1, 0, f), y_r.at[0, f])
        kv_pass(1, f)

    kv_far(1)
    kv_far(3)
    kv_two(0, 0)
    kv_two(2, 3)
    kv_far(2)
    kv_core(0, 0)
    weight_wait(0, 1)
    weight_send(0, 3)

    for d in range(1, 16):
        from_z = lax.rem(z + 16 - d, 16)
        arrived(qrecv.at[pl.ds(from_z * 16, 16)], q_r.at[d])
    lane = iota((STEPS, 256), 1)
    for which in range(2):
        o_y = yh if which == 0 else 1 - yh
        spots = rows_of(STEPS, o_y * 16 + z).astype(I32)
        source = spots >> 7
        diagonal = iota((STEPS, STEPS), 0) == iota((STEPS, STEPS), 1)
        source_row = jnp.sum(
            jnp.where(diagonal, source.astype(F32), 0.0), axis=0, keepdims=True
        ).astype(I32)
        earlier = iota((STEPS, STEPS), 1) < iota((STEPS, STEPS), 0)
        rank = jnp.sum(
            jnp.where((source == source_row) & earlier, 1.0, 0.0), axis=1, keepdims=True
        ).astype(I32)
        for h in range(2):
            wanted = (source & 15) * 16 + o_y * 8 + h * 4 + rank
            take = ((wanted == lane) & (source >> 4 == yh)).astype(BF16)
            rows = nn(take, qrecv[...]).astype(BF16)
            if which == 0:
                qall[h * 160 + TOK : (h + 1) * 160] = rows
            else:
                qmid_s[h * STEPS : (h + 1) * STEPS] = rows
    send(qmid_s, qmid_r, qm_s, qm_r, partner)

    state = [jnp.full((320, 1), MASKED, F32), jnp.zeros((320, 1), F32), jnp.zeros((320, HD), F32)]

    def attend(p, n):
        py = yh if p == 0 else 1 - yh
        set_ = lax.rem(zr + (0, 3, 1, 2)[n], 4)
        arrived(kv_bundle(p, n, 1 - core), c_r.at[p, n])
        keys = kv[0, py, set_].reshape(512, HD)
        values = kv[1, py, set_].reshape(512, HD)
        highest, totals, accum = state
        scores = nt(qall[...], keys) * (HD**-0.5)
        kk = iota((320, 512), 1)
        spot = (py * 16 + set_) * TOK + (kk >> 7) * 512 + (kk & 127)
        scores = jnp.where(spot <= posc[:, 0:1], scores, MASKED)
        new = jnp.maximum(highest, jnp.max(scores, axis=1, keepdims=True))
        alpha = jnp.exp(highest - new)
        weights = jnp.exp(scores - new)
        state[0] = new
        state[1] = totals * alpha + jnp.sum(weights, axis=1, keepdims=True)
        state[2] = accum * alpha + nn(weights.astype(BF16), values)

    kv_other(1)
    kv_other(3)
    kv_two(1, 1)
    kv_two(3, 2)
    kv_core(0, 3)
    kv_other(2)
    kv_core(1, 0)
    arrived(qmid_r, qm_r)
    for h in range(2):
        rows = slice(h * 160 + TOK, (h + 1) * 160)
        qall[rows] = (
            qall[rows].astype(F32) + qmid_r[h * STEPS : (h + 1) * STEPS].astype(F32)
        ).astype(BF16)
    arrived(rmid, m_r)
    for g in range(4):
        either(rmid.at[pl.ds(g * 32, 32)], rbuf.at[held_half, par], r_s.at[g], r_r.at[held_half, par], res_dest(g))

    attend(0, 0)
    for n in (1, 2):
        for f in range(4):
            arrived(kv_block(0, n, f), near_r.at[0, n, f])
        kv_core(0, n)
    attend(1, 0)
    attend(0, 3)
    for n in (1, 2):
        for f in range(4):
            arrived(kv_block(1, n, f), near_r.at[1, n, f])
        kv_core(1, n)

    for bundle in ((0, 1), (0, 2), (1, 1)):
        attend(*bundle)
    for f in range(4):
        arrived(kv_block(1, 3, f), y_r.at[1, f])
    kv_core(1, 3)
    attend(1, 2)
    attend(1, 3)
    mixed = (state[2] / state[1]).astype(BF16)
    k_rows = pl.ds(pl.multiple_of(pair * STEPS, STEPS), STEPS)
    for h in range(2):
        agrp[k_rows, h * HD : (h + 1) * HD] = mixed[h * 160 + TOK : (h + 1) * 160]

    for d in (4, 3, 5, 2, 6, 1, 7):
        send(agrp.at[k_rows], agrp.at[k_rows], a_s.at[d], a_r.at[d], zdev(2 * d))
    for h in range(2):
        att_ref[:, h * HD : (h + 1) * HD] = mixed[h * 160 : h * 160 + TOK]

    for d in range(1, 16):
        src_t = lax.rem(t + 16 - d, 16)
        arrived(gbuf.at[src_t], g_r.at[d])
    gain = nn(gbuf[pair], shift(320, COLS, 0)) + nn(gbuf[8 + pair], shift(320, COLS, 320))
    gain = gain[0:1]
    for j in range(2):
        for s in range(2):
            arrived(rbuf.at[j, s], r_r.at[j, s])
    row = iota((256, 1), 0)
    spots = rows_of(256, yh * 16 + 2 * (iota((256, 128), 0) >> 5) + par).astype(I32)
    step = (row & 31) * 32 + yh * 16 + 2 * (row >> 5) + par
    slot = iota((256, 64), 1)
    res_part = jnp.zeros((256, COLS), F32)
    for j in range(2):
        source = res_source(j) * 16 + 2 * res_pair
        nth = (spots >> 7) - source
        rank = (step - jnp.where(nth == 0, before(source * TOK), before((source + 1) * TOK))) >> 5
        wanted = jnp.where((nth == 0) | (nth == 1), nth * 32 + (row >> 5) * 4 + rank, 1000)
        rows = nn((wanted == slot).astype(BF16), rbuf[j].reshape(64, 320)).astype(BF16)
        res_part += nn(rows, shift(320, COLS, j * 320))

    res_add[...] = res_part

    weight_wait(0, 2)
    weight_wait(0, 3)
    for d in range(1, 8):
        from_k = lax.rem(pair + 8 - d, 8)
        arrived(agrp.at[pl.ds(pl.multiple_of(from_k * STEPS, STEPS), STEPS)], a_r.at[d])
    mine = pl.ds(pl.multiple_of(core * 128, 128), 128)
    theirs = pl.ds(pl.multiple_of((1 - core) * 128, 128), 128)
    chip = t // 2
    pb[...] = (nt(agrp[theirs], wob[...]) + res_add[theirs]).astype(BF16)
    send(pb, px, x_s.at[0], x_r.at[0], other_core)
    partial = nt(agrp[mine], wob[...]) + res_add[mine]
    arrived(px, x_r.at[0])
    ph[...] = (partial + px[...].astype(F32)).astype(BF16)

    def chip_rows(index):
        return pl.ds(pl.multiple_of(index * 16, 16), 16)

    for d in (4, 3, 5, 2, 6, 1, 7):
        send(ph.at[chip_rows(lax.rem(chip + d, 8))], rb.at[chip], p_s.at[d], p_r.at[d], tdev(2 * d))
    weight_send(1, 1)
    total = ph[chip_rows(chip)].astype(F32)
    for d in range(1, 8):
        src = lax.rem(chip + 8 - d, 8)
        arrived(rb.at[src], p_r.at[d])
        total += rb[src].astype(F32)
    own_rows = chip_rows(core * 8 + chip)
    sb[own_rows] = total.astype(BF16)
    for d in (4, 3, 5, 2, 6, 1, 7):
        send(sb.at[own_rows], sb.at[own_rows], s_s.at[d], s_r.at[d], tdev(2 * d))
    weight_wait(1, 1)
    weight_send(1, 3)
    weight_wait(1, 2)
    for d in range(1, 8):
        arrived(sb.at[chip_rows(core * 8 + lax.rem(chip + 8 - d, 8))], s_r.at[d])
    send(sb.at[mine], sb.at[mine], x_s.at[1], x_r.at[1], other_core)
    weight_wait(1, 3)
    wmbig[...] = nn(wmb[...], shift(320, 384, 0)).astype(BF16)

    def score(rows, first_owner):
        states = sb[rows].astype(F32)
        squares = jnp.sum(states * states, axis=1, keepdims=True)
        pre = nn((states * gain).astype(BF16), wmbig[...])
        sq_hi = squares.astype(BF16).astype(F32)
        col = iota((128, 384), 1)
        pre = jnp.where(col == 320, sq_hi, jnp.where(col == 321, squares - sq_hi, pre))
        yb[rows] = pre.astype(BF16)
        nearby = pair // 4 == first_owner // 4
        for far, near in ((0, 2), (1, 3), (3, 1), (2, 0)):
            k = first_owner + lax.rem(pair + jnp.where(nearby, near, far), 4)
            piece = yb.at[pl.ds(pl.multiple_of(k * STEPS, STEPS), STEPS)]

            @pl.when(k != pair)
            def _(k=k, piece=piece):
                pltpu.make_async_remote_copy(
                    src_ref=piece, dst_ref=yr.at[pair], send_sem=z_s.at[k], recv_sem=z_r.at[pair],
                    device_id=(yh * 16 + 2 * k + par, t), device_id_type=MESH,
                ).start()

    score(mine, core * 4)
    arrived(sb.at[theirs], x_r.at[1])
    score(theirs, (1 - core) * 4)

    out_k = lax.rem(slot_t + 3 * pair, 8)
    block = sb[pl.ds(pl.multiple_of(out_k * STEPS, STEPS), STEPS)]
    ob_s[...] = nn(
        block, (iota((COLS, 320), 0) == iota((COLS, 320), 1) + half_t * 320).astype(BF16)
    ).astype(BF16)

    out_z = (yh * 16 + 2 * out_k + par, t)
    out_t = (c, half_t * 8 + lax.rem(3 * (pair + 8 - slot_t), 8))
    either(ob_s, ob_z, o_s.at[0], o_r.at[0], out_z)

    yr[pair] = yb[k_rows]
    for k in range(8):

        @pl.when(k != pair)
        def _(k=k):
            arrived(yr.at[k], z_r.at[k])

    total = yr[0].astype(F32)
    for k in range(1, 8):
        total += yr[k].astype(F32)
    col = iota((STEPS, 384), 1)
    squares = jnp.sum(jnp.where((col == 320) | (col == 321), total, 0.0), axis=1, keepdims=True)
    pre = jnp.where(col < 320, total * lax.rsqrt(squares / D + 1e-06), 0.0)
    hidden = (pre / (1.0 + jnp.exp(-pre))).astype(BF16)
    fb[...] = nt(lwt[...], hidden)
    for d in range(1, 16):
        to_t = lax.rem(t + d, 16)
        send(fb.at[pl.ds(pl.multiple_of(to_t * 8, 8), 8)], fr.at[t], f_s.at[d], f_r.at[d], tdev(d))
    arrived(ob_z, o_r.at[0])
    either(ob_z, ob, o_s.at[1], o_r.at[1], out_t)
    total = fb[pl.ds(pl.multiple_of(t * 8, 8), 8)]
    for d in range(1, 16):
        src_t = lax.rem(t + 16 - d, 16)
        arrived(fr.at[src_t], f_r.at[d])
        total += fr[src_t]
    levels_ref[...] = total
    arrived(ob, o_r.at[1])
    states_ref[...] = ob[...]

    for copy in sends:
        copy.wait_send()
    either_sent(rsend, m_s, res_mid)
    for g in range(4):
        either_sent(rmid.at[pl.ds(g * 32, 32)], r_s.at[g], res_dest(g))

    for k in range(8):

        @pl.when(k != pair)
        def _(k=k):
            arrived(yr.at[k], z_s.at[k])

    either_sent(ob_s, o_s.at[0], out_z)
    either_sent(ob_z, o_s.at[1], out_t)


def on_device(q, k, v, res, wo, gain, wm, lw, positions):
    vmem = pl.BlockSpec(memory_space=pltpu.VMEM)
    dma = pltpu.SemaphoreType.DMA
    scratch = [
        pltpu.VMEM((320, TOK), BF16),
        pltpu.VMEM((320,), BF16),
        pltpu.VMEM((320, 128), BF16),
        pltpu.VMEM((8, 128), I32),
        pltpu.VMEM((2, 2, 4, 4, TOK, HD), BF16),
        pltpu.VMEM((320, HD), BF16),
        pltpu.VMEM((256, HD), BF16),
        pltpu.VMEM((256, HD), BF16),
        pltpu.VMEM((64, HD), BF16),
        pltpu.VMEM((64, HD), BF16),
        pltpu.VMEM((320, 128), I32),
        pltpu.VMEM((128, 320), BF16),
        pltpu.VMEM((128, 320), BF16),
        pltpu.VMEM((2, 2, 32, 320), BF16),
        pltpu.VMEM((16, 16, 320), BF16),
        pltpu.VMEM((COLS, 256), BF16),
        pltpu.VMEM((COLS, 320), BF16),
        pltpu.VMEM((COLS, 384), BF16),
        pltpu.VMEM((128, 384), BF16),
        pltpu.VMEM((256, 256), BF16),
        pltpu.VMEM((256, COLS), F32),
        pltpu.VMEM((128, COLS), BF16),
        pltpu.VMEM((128, COLS), BF16),
        pltpu.VMEM((128, COLS), BF16),
        pltpu.VMEM((8, 16, COLS), BF16),
        pltpu.VMEM((256, COLS), BF16),
        pltpu.VMEM((32, 320), BF16),
        pltpu.VMEM((32, 320), BF16),
        pltpu.VMEM((32, 320), BF16),
        pltpu.VMEM((256, 384), BF16),
        pltpu.VMEM((8, 32, 384), BF16),
        pltpu.VMEM((128, 32), F32),
        pltpu.VMEM((16, 8, 32), F32),
        dma((9,)), dma((4,)), dma((4,)), dma((2, 4, 4)), dma((2, 4, 4)), dma((2, 4)), dma((2, 4)), dma((2, 4)), dma((2, 4)),
        dma((16,)), dma((16,)), dma(()), dma(()), dma(()), dma(()), dma((4,)), dma((2, 2)), dma((16,)), dma((16,)), dma((2, 4)), dma((2, 4)),
        dma((8,)), dma((8,)), dma((2,)), dma((2,)), dma((8,)), dma((8,)), dma((8,)), dma((8,)), dma((2,)), dma((2,)), dma((8,)), dma((8,)), dma((16,)), dma((16,)),
    ]
    attended, states, levels = pl.pallas_call(
        kernel,
        out_shape=(
            jax.ShapeDtypeStruct((TOK, 2 * HD), BF16),
            jax.ShapeDtypeStruct((STEPS, 320), BF16),
            jax.ShapeDtypeStruct((8, STEPS), F32),
        ),
        in_specs=[pl.BlockSpec(memory_space=pltpu.HBM)] * 9,
        out_specs=(vmem, vmem, vmem),
        scratch_shapes=scratch,
        compiler_params=pltpu.CompilerParams(
            collective_id=0, has_side_effects=True, vmem_limit_bytes=(54 * 1024 - 256) * 1024
        ),
    )(q, k, v, res.T, wo.T, gain, wm, lw, positions.reshape(8, 128))
    return attended, states, levels.T


def solution(mesh):
    in_specs = (
        P("ctx", "tp"),
        P("ctx", None),
        P("ctx", None),
        P("ctx", "tp"),
        P("tp", "ctx"),
        P("tp"),
        P("ctx", "tp"),
        P("tp", None),
        P(),
    )
    out_specs = (P("ctx", "tp"), P("ctx", "tp"), P("ctx", "tp"))
    return jax.shard_map(
        on_device, mesh=mesh, in_specs=in_specs, out_specs=out_specs, check_vma=False
    )
```

```python
import functools

import jax
import jax.numpy as jnp
from jax import lax
from jax.experimental import pallas as pl
from jax.experimental.pallas import tpu as pltpu
from jax.sharding import PartitionSpec as P

D = 5120
HD = 128
TOK = 128
STEPS = 32
COLS = 640
MASKED = -1e30
MESH = pl.DeviceIdType.MESH
F32 = jnp.float32
BF16 = jnp.bfloat16
I32 = jnp.int32


def iota(shape, dim):
    return lax.broadcasted_iota(I32, shape, dim)


def nn(a, b):
    return lax.dot_general(a, b, (((1,), (0,)), ((), ())), preferred_element_type=F32)


def nt(a, b):
    return lax.dot_general(a, b, (((1,), (1,)), ((), ())), preferred_element_type=F32)


def tn(a, b):
    return lax.dot_general(a, b, (((0,), (0,)), ((), ())), preferred_element_type=F32)


def shift(rows, cols, offset):
    return (iota((rows, cols), 0) + offset == iota((rows, cols), 1)).astype(BF16)


def kernel(
    q_hbm, k_hbm, v_hbm, res_hbm, wo_hbm, gain_hbm, wm_hbm, lw_hbm, pos_hbm,
    att_ref, states_ref, levels_ref,
    res_ref, gain_ref, lw_ref, pos_ref, kv, qall, qsend, qrecv, qmid_s, qmid_r, posc,
    rsend, rmid, rbuf, gbuf, wob, wmb, wmbig, lwt,
    agrp, res_add, pb, px, ph, rb, sb, ob_s, ob_z, ob, yb, yr, fb, fr,
    in_s, far_s, far_r, near_s, near_r, y_s, y_r, c_s, c_r,
    q_s, q_r, qm_s, qm_r, m_s, m_r, r_s, r_r, g_s, g_r, w_s, w_r,
    a_s, a_r, x_s, x_r, p_s, p_r, s_s, s_r, o_s, o_r, z_s, z_r, f_s, f_r,
):
    c = lax.axis_index("ctx")
    t = lax.axis_index("tp")
    z = lax.rem(c, 16)
    yh = c // 16
    core = lax.rem(t, 2)
    group = t // 2
    par = lax.rem(z, 2)
    mate_z = z + 1 - 2 * par
    pair = z // 2
    zr = lax.rem(z, 4)
    zq = z // 4
    partner = ((1 - yh) * 16 + z, t)
    other_core = (c, t + 1 - 2 * core)
    sends = []

    def zdev(d):
        return (yh * 16 + lax.rem(z + 16 + d, 16), t)

    def tdev(d):
        return (c, lax.rem(t + d, 16))

    def send(src, dst, ssem, rsem, dev):
        copy = pltpu.make_async_remote_copy(
            src_ref=src, dst_ref=dst, send_sem=ssem, recv_sem=rsem, device_id=dev, device_id_type=MESH
        )
        copy.start()
        sends.append(copy)

    def elsewhere(dev):
        return jnp.logical_not((dev[0] == c) & (dev[1] == t))

    def either(src, dst, ssem, rsem, dev):
        @pl.when(elsewhere(dev))
        def _():
            pltpu.make_async_remote_copy(
                src_ref=src, dst_ref=dst, send_sem=ssem, recv_sem=rsem, device_id=dev, device_id_type=MESH
            ).start()

        @pl.when(jnp.logical_not(elsewhere(dev)))
        def _():
            pltpu.make_async_copy(src, dst, rsem).start()

    def either_sent(src, ssem, dev):
        @pl.when(elsewhere(dev))
        def _():
            arrived(src, ssem)

    def arrived(dst, rsem):
        pltpu.make_async_copy(dst, dst, rsem).wait()

    barrier = pltpu.get_barrier_semaphore()

    def greet(dev):
        pl.semaphore_signal(barrier, inc=1, device_id=dev, device_id_type=MESH)

    for d in range(1, 16):
        greet(zdev(d))
        greet(tdev(d))
    greet(partner)
    greet(((1 - yh) * 16 + mate_z, t))
    half_t, slot_t = t // 8, lax.rem(t, 8)
    res_mid = (c, lax.rem(yh + half_t, 2) * 8 + lax.rem(slot_t + 64 - 3 * pair, 8))
    held_pair = lax.rem(slot_t + 3 * pair, 8)
    held_half = lax.rem(half_t + yh, 2)
    res_pair = lax.rem(3 * (pair + 8 - slot_t), 8)

    def res_dest(g):
        return ((g // 2) * 16 + 2 * held_pair + g % 2, t)

    def res_source(j):
        return lax.rem(half_t + j, 2)

    res_peers = [res_dest(g) for g in range(4)] + [
        (res_source(j) * 16 + 2 * res_pair + p, t) for j in range(2) for p in range(2)
    ]
    n_peers = 32
    for dev in res_peers:
        n_peers += jnp.where(elsewhere(dev), 1, 0)

        @pl.when(elsewhere(dev))
        def _(dev=dev):
            greet(dev)

    w_here = yh * 2 + par
    wo_rows = pl.ds(pl.multiple_of(w_here * 160, 16), 160)
    lanes = pl.ds(pl.multiple_of(group * HD, HD), HD)
    here = kv.at[core, yh, zr, zq]
    fetches = [
        pltpu.make_async_copy(pos_hbm, pos_ref, in_s.at[0]),
        pltpu.make_async_copy(q_hbm.at[:, pl.ds(0, HD)], qall.at[pl.ds(0, TOK)], in_s.at[1]),
        pltpu.make_async_copy(q_hbm.at[:, pl.ds(HD, HD)], qall.at[pl.ds(160, TOK)], in_s.at[2]),
        pltpu.make_async_copy(res_hbm, res_ref, in_s.at[3]),
        pltpu.make_async_copy(gain_hbm, gain_ref, in_s.at[4]),
        pltpu.make_async_copy(lw_hbm, lw_ref, in_s.at[5]),
        pltpu.make_async_copy(wo_hbm, wob.at[wo_rows], in_s.at[6]),
        pltpu.make_async_copy(wm_hbm, wmb.at[wo_rows], in_s.at[7]),
    ]

    @pl.when(core == 0)
    def _():
        pltpu.make_async_copy(k_hbm.at[:, lanes], here, in_s.at[8]).start()

    @pl.when(core == 1)
    def _():
        pltpu.make_async_copy(v_hbm.at[:, lanes], here, in_s.at[8]).start()

    for fetch in fetches:
        fetch.start()

    fetches[0].wait()
    pos8 = pos_ref[...]
    hi8 = (pos8 >> 6).astype(F32).astype(BF16)
    lo8 = (pos8 & 63).astype(F32).astype(BF16)
    eye128 = shift(128, 128, 0)
    base = c * TOK

    def before(limit):
        hits = jnp.where(pos8 < limit, 1.0, 0.0)
        return jnp.sum(jnp.sum(hits, axis=1, keepdims=True), axis=0, keepdims=True).astype(I32)

    first = before(base)
    selq = jnp.zeros((256, TOK), F32)
    slot_q = iota((256, 128), 0)
    key_q = (((slot_q >> 3) & 1) * 16 + (slot_q >> 4)) * 4 + (slot_q & 3)

    def held_steps(a):
        spot = pos8[a : a + 1]
        step = iota((1, 128), 1) + a * 128
        here_too = (spot >= base) & (spot < base + TOK)
        key = jnp.where(here_too, (step & 31) * 4 + ((step - first) >> 5), -1)
        return key, (spot == iota((TOK, 128), 0) + base).astype(BF16)

    for a in range(8):
        key, held = held_steps(a)
        selq += nt((key == key_q).astype(BF16), held)
    selq = selq.astype(BF16)
    head_row = (iota((256, 128), 0) >> 2) & 1
    fetches[1].wait()
    fetches[2].wait()
    qsend[...] = jnp.where(
        head_row == 0, nn(selq, qall[0:TOK]), nn(selq, qall[160 : 160 + TOK])
    ).astype(BF16)

    def rows_of(count, owner):
        pick = ((iota((count, 8), 0) & 31) >> 2 == iota((count, 8), 1)).astype(BF16)
        spread = nn(pick, hi8) * 64.0 + nn(pick, lo8)
        lane = (iota((count, 128), 0) & 3) * 32 + owner
        return jnp.sum(jnp.where(iota((count, 128), 1) == lane, spread, 0.0), axis=1, keepdims=True)

    pl.semaphore_wait(barrier, n_peers)

    arrived(here, in_s.at[8])

    def kv_block(plane, n, f):
        py = yh if plane == 0 else 1 - yh
        from_z = lax.rem(z + (0, 15, 1, 14)[n] + 16 - 4 * f, 16)
        return kv.at[core, py, lax.rem(from_z, 4), from_z // 4]

    def kv_bundle(plane, n, kind):
        py = yh if plane == 0 else 1 - yh
        return kv.at[kind, py, lax.rem(zr + (0, 3, 1, 2)[n], 4)]

    def kv_pass(plane, f):
        block = kv_block(plane, 0, f)
        if plane == 0:
            if f in (0, 1):
                send(block, block, near_s.at[0, 3, f], near_r.at[0, 3, f], zdev(2))
            if f in (0, 3):
                send(block, block, near_s.at[0, 3, 2 + f // 3], near_r.at[0, 3, 2 + f // 3], zdev(-2))
        for n, d in ((1, 1), (2, -1)):
            send(block, block, near_s.at[plane, n, f], near_r.at[plane, n, f], zdev(d))

    def kv_cross(n, f):
        block = kv_block(0, n, f)
        send(block, block, y_s.at[n // 3, f], y_r.at[n // 3, f], partner)

    def kv_core(plane, n):
        bundle = kv_bundle(plane, n, core)
        send(bundle, bundle, c_s.at[plane, n], c_r.at[plane, n], other_core)

    def weight_rows(r):
        slot = (yh if r < 2 else 1 - yh) * 2 + (par if r % 2 == 0 else 1 - par)
        return pl.ds(pl.multiple_of(slot * 160, 16), 160)

    def weight_send(w, r):
        buffer = (wob, wmb)[w]
        rows = weight_rows(1) if r == 3 else wo_rows
        dev = (yh * 16 + mate_z, t) if r == 1 else partner
        send(buffer.at[rows], buffer.at[rows], w_s.at[w, r], w_r.at[w, r], dev)

    def weight_wait(w, r):
        arrived((wob, wmb)[w].at[weight_rows(r)], w_r.at[w, r])

    for f in (2, 1, 3):
        send(here, here, far_s.at[f], far_r.at[f], zdev(4 * f))
    kv_cross(0, 0)
    for d in (8, 7, 9, 6, 10, 5, 11, 4, 12, 3, 13, 2, 14, 1, 15):
        zd = lax.rem(z + d, 16)
        send(
            qsend.at[pl.ds(zd * 16, 16)], qrecv.at[pl.ds(z * 16, 16)], q_s.at[d], q_r.at[d], zdev(d)
        )
    qrecv[pl.ds(pl.multiple_of(z * 16, 16), 16)] = qsend[pl.ds(pl.multiple_of(z * 16, 16), 16)]
    kv_pass(0, 0)
    fetches[6].wait()
    weight_send(0, 2)
    fetches[7].wait()
    weight_send(1, 2)
    weight_send(0, 1)
    mine = rows_of(STEPS, c)
    for h in range(2):
        posc[h * 160 : h * 160 + TOK] = iota((TOK, 128), 0) + base
        posc[h * 160 + TOK : (h + 1) * 160] = jnp.broadcast_to(mine.astype(I32), (STEPS, 128))
    selr = jnp.zeros((128, TOK), F32)
    slot_r = iota((128, 128), 0)
    key_r = ((slot_r >> 6) * 16 + ((slot_r >> 2) & 7) * 2 + ((slot_r >> 5) & 1)) * 4 + (slot_r & 3)
    for a in range(8):
        key, held = held_steps(a)
        selr += nt((key == key_r).astype(BF16), held)
    fetches[3].wait()
    rsend[...] = nt(selr.astype(BF16), res_ref[...]).astype(BF16)
    fetches[4].wait()
    either(rsend, rmid, m_s, m_r, res_mid)
    gbuf[t] = jnp.broadcast_to(gain_ref[...].astype(F32).reshape(1, 320), (16, 320)).astype(BF16)
    for d in range(1, 16):
        send(gbuf.at[t], gbuf.at[t], g_s.at[d], g_r.at[d], tdev(d))
    fetches[5].wait()
    lwt[...] = nn(nt(eye128, lw_ref[...]).astype(BF16), shift(320, 384, 0)).astype(BF16)

    arrived(kv_block(1, 0, 0), y_r.at[0, 0])
    kv_pass(1, 0)

    def kv_far(f):
        arrived(kv_block(0, 0, f), far_r.at[f])
        kv_cross(0, f)
        kv_pass(0, f)

    def kv_two(i, f):
        arrived(kv_block(0, 3, f), near_r.at[0, 3, i])
        kv_cross(3, f)

    def kv_other(f):
        arrived(kv_block(1, 0, f), y_r.at[0, f])
        kv_pass(1, f)

    kv_far(1)
    kv_far(3)
    kv_two(0, 0)
    kv_two(2, 3)
    kv_far(2)
    kv_core(0, 0)
    weight_wait(0, 1)
    weight_send(0, 3)

    for d in range(1, 16):
        from_z = lax.rem(z + 16 - d, 16)
        arrived(qrecv.at[pl.ds(from_z * 16, 16)], q_r.at[d])
    lane = iota((STEPS, 256), 1)
    for which in range(2):
        o_y = yh if which == 0 else 1 - yh
        spots = rows_of(STEPS, o_y * 16 + z).astype(I32)
        source = spots >> 7
        diagonal = iota((STEPS, STEPS), 0) == iota((STEPS, STEPS), 1)
        source_row = jnp.sum(
            jnp.where(diagonal, source.astype(F32), 0.0), axis=0, keepdims=True
        ).astype(I32)
        earlier = iota((STEPS, STEPS), 1) < iota((STEPS, STEPS), 0)
        rank = jnp.sum(
            jnp.where((source == source_row) & earlier, 1.0, 0.0), axis=1, keepdims=True
        ).astype(I32)
        for h in range(2):
            wanted = (source & 15) * 16 + o_y * 8 + h * 4 + rank
            take = ((wanted == lane) & (source >> 4 == yh)).astype(BF16)
            rows = nn(take, qrecv[...]).astype(BF16)
            if which == 0:
                qall[h * 160 + TOK : (h + 1) * 160] = rows
            else:
                qmid_s[h * STEPS : (h + 1) * STEPS] = rows
    send(qmid_s, qmid_r, qm_s, qm_r, partner)

    state = [jnp.full((320, 1), MASKED, F32), jnp.zeros((320, 1), F32), jnp.zeros((320, HD), F32)]

    def attend(p, n):
        py = yh if p == 0 else 1 - yh
        set_ = lax.rem(zr + (0, 3, 1, 2)[n], 4)
        arrived(kv_bundle(p, n, 1 - core), c_r.at[p, n])
        keys = kv[0, py, set_].reshape(512, HD)
        values = kv[1, py, set_].reshape(512, HD)
        highest, totals, accum = state
        scores = nt(qall[...], keys) * (HD**-0.5)
        kk = iota((320, 512), 1)
        spot = (py * 16 + set_) * TOK + (kk >> 7) * 512 + (kk & 127)
        scores = jnp.where(spot <= posc[:, 0:1], scores, MASKED)
        new = jnp.maximum(highest, jnp.max(scores, axis=1, keepdims=True))
        alpha = jnp.exp(highest - new)
        weights = jnp.exp(scores - new)
        state[0] = new
        state[1] = totals * alpha + jnp.sum(weights, axis=1, keepdims=True)
        state[2] = accum * alpha + nn(weights.astype(BF16), values)

    kv_other(1)
    kv_other(3)
    kv_two(1, 1)
    kv_two(3, 2)
    kv_core(0, 3)
    kv_other(2)
    kv_core(1, 0)
    arrived(qmid_r, qm_r)
    for h in range(2):
        rows = slice(h * 160 + TOK, (h + 1) * 160)
        qall[rows] = (
            qall[rows].astype(F32) + qmid_r[h * STEPS : (h + 1) * STEPS].astype(F32)
        ).astype(BF16)
    arrived(rmid, m_r)
    for g in range(4):
        either(rmid.at[pl.ds(g * 32, 32)], rbuf.at[held_half, par], r_s.at[g], r_r.at[held_half, par], res_dest(g))

    attend(0, 0)
    for n in (1, 2):
        for f in range(4):
            arrived(kv_block(0, n, f), near_r.at[0, n, f])
        kv_core(0, n)
    attend(1, 0)
    attend(0, 3)
    for n in (1, 2):
        for f in range(4):
            arrived(kv_block(1, n, f), near_r.at[1, n, f])
        kv_core(1, n)

    weight_send(1, 1)
    for bundle in ((0, 1), (0, 2), (1, 1)):
        attend(*bundle)
    for f in range(4):
        arrived(kv_block(1, 3, f), y_r.at[1, f])
    kv_core(1, 3)
    attend(1, 2)
    attend(1, 3)
    mixed = (state[2] / state[1]).astype(BF16)
    k_rows = pl.ds(pl.multiple_of(pair * STEPS, STEPS), STEPS)
    for h in range(2):
        agrp[k_rows, h * HD : (h + 1) * HD] = mixed[h * 160 + TOK : (h + 1) * 160]

    for d in (4, 3, 5, 2, 6, 1, 7):
        send(agrp.at[k_rows], agrp.at[k_rows], a_s.at[d], a_r.at[d], zdev(2 * d))
    for h in range(2):
        att_ref[:, h * HD : (h + 1) * HD] = mixed[h * 160 : h * 160 + TOK]

    weight_wait(1, 1)
    weight_send(1, 3)
    for d in range(1, 16):
        src_t = lax.rem(t + 16 - d, 16)
        arrived(gbuf.at[src_t], g_r.at[d])
    gain = nn(gbuf[pair], shift(320, COLS, 0)) + nn(gbuf[8 + pair], shift(320, COLS, 320))
    gain = gain[0:1]
    for j in range(2):
        for s in range(2):
            arrived(rbuf.at[j, s], r_r.at[j, s])
    row = iota((256, 1), 0)
    spots = rows_of(256, yh * 16 + 2 * (iota((256, 128), 0) >> 5) + par).astype(I32)
    step = (row & 31) * 32 + yh * 16 + 2 * (row >> 5) + par
    slot = iota((256, 64), 1)
    res_part = jnp.zeros((256, COLS), F32)
    for j in range(2):
        source = res_source(j) * 16 + 2 * res_pair
        nth = (spots >> 7) - source
        rank = (step - jnp.where(nth == 0, before(source * TOK), before((source + 1) * TOK))) >> 5
        wanted = jnp.where((nth == 0) | (nth == 1), nth * 32 + (row >> 5) * 4 + rank, 1000)
        rows = nn((wanted == slot).astype(BF16), rbuf[j].reshape(64, 320)).astype(BF16)
        res_part += nn(rows, shift(320, COLS, j * 320))

    res_add[...] = res_part

    weight_wait(0, 2)
    weight_wait(0, 3)
    for d in range(1, 8):
        from_k = lax.rem(pair + 8 - d, 8)
        arrived(agrp.at[pl.ds(pl.multiple_of(from_k * STEPS, STEPS), STEPS)], a_r.at[d])
    mine = pl.ds(pl.multiple_of(core * 128, 128), 128)
    theirs = pl.ds(pl.multiple_of((1 - core) * 128, 128), 128)
    chip = t // 2
    pb[...] = (nt(agrp[theirs], wob[...]) + res_add[theirs]).astype(BF16)
    send(pb, px, x_s.at[0], x_r.at[0], other_core)
    partial = nt(agrp[mine], wob[...]) + res_add[mine]
    arrived(px, x_r.at[0])
    ph[...] = (partial + px[...].astype(F32)).astype(BF16)

    def chip_rows(index):
        return pl.ds(pl.multiple_of(index * 16, 16), 16)

    for d in (4, 3, 5, 2, 6, 1, 7):
        send(ph.at[chip_rows(lax.rem(chip + d, 8))], rb.at[chip], p_s.at[d], p_r.at[d], tdev(2 * d))
    weight_wait(1, 2)
    weight_wait(1, 3)
    wmbig[...] = nn(wmb[...], shift(320, 384, 0)).astype(BF16)
    total = ph[chip_rows(chip)].astype(F32)
    for d in range(1, 8):
        src = lax.rem(chip + 8 - d, 8)
        arrived(rb.at[src], p_r.at[d])
        total += rb[src].astype(F32)
    own_rows = chip_rows(core * 8 + chip)
    sb[own_rows] = total.astype(BF16)
    for d in (4, 3, 5, 2, 6, 1, 7):
        send(sb.at[own_rows], sb.at[own_rows], s_s.at[d], s_r.at[d], tdev(2 * d))
    for d in range(1, 8):
        arrived(sb.at[chip_rows(core * 8 + lax.rem(chip + 8 - d, 8))], s_r.at[d])
    send(sb.at[mine], sb.at[mine], x_s.at[1], x_r.at[1], other_core)

    def score(rows, first_owner):
        states = sb[rows].astype(F32)
        squares = jnp.sum(states * states, axis=1, keepdims=True)
        pre = nn((states * gain).astype(BF16), wmbig[...])
        sq_hi = squares.astype(BF16).astype(F32)
        col = iota((128, 384), 1)
        pre = jnp.where(col == 320, sq_hi, jnp.where(col == 321, squares - sq_hi, pre))
        yb[rows] = pre.astype(BF16)
        nearby = pair // 4 == first_owner // 4
        for far, near in ((0, 2), (1, 3), (3, 1), (2, 0)):
            k = first_owner + lax.rem(pair + jnp.where(nearby, near, far), 4)
            piece = yb.at[pl.ds(pl.multiple_of(k * STEPS, STEPS), STEPS)]

            @pl.when(k != pair)
            def _(k=k, piece=piece):
                pltpu.make_async_remote_copy(
                    src_ref=piece, dst_ref=yr.at[pair], send_sem=z_s.at[k], recv_sem=z_r.at[pair],
                    device_id=(yh * 16 + 2 * k + par, t), device_id_type=MESH,
                ).start()

    score(mine, core * 4)
    arrived(sb.at[theirs], x_r.at[1])
    score(theirs, (1 - core) * 4)

    out_k = lax.rem(slot_t + 3 * pair, 8)
    block = sb[pl.ds(pl.multiple_of(out_k * STEPS, STEPS), STEPS)]
    ob_s[...] = nn(
        block, (iota((COLS, 320), 0) == iota((COLS, 320), 1) + half_t * 320).astype(BF16)
    ).astype(BF16)

    out_z = (yh * 16 + 2 * out_k + par, t)
    out_t = (c, half_t * 8 + lax.rem(3 * (pair + 8 - slot_t), 8))
    either(ob_s, ob_z, o_s.at[0], o_r.at[0], out_z)

    yr[pair] = yb[k_rows]
    for k in range(8):

        @pl.when(k != pair)
        def _(k=k):
            arrived(yr.at[k], z_r.at[k])

    total = yr[0].astype(F32)
    for k in range(1, 8):
        total += yr[k].astype(F32)
    col = iota((STEPS, 384), 1)
    squares = jnp.sum(jnp.where((col == 320) | (col == 321), total, 0.0), axis=1, keepdims=True)
    pre = jnp.where(col < 320, total * lax.rsqrt(squares / D + 1e-06), 0.0)
    hidden = (pre / (1.0 + jnp.exp(-pre))).astype(BF16)
    fb[...] = nt(lwt[...], hidden)
    for d in range(1, 16):
        to_t = lax.rem(t + d, 16)
        send(fb.at[pl.ds(pl.multiple_of(to_t * 8, 8), 8)], fr.at[t], f_s.at[d], f_r.at[d], tdev(d))
    arrived(ob_z, o_r.at[0])
    either(ob_z, ob, o_s.at[1], o_r.at[1], out_t)
    total = fb[pl.ds(pl.multiple_of(t * 8, 8), 8)]
    for d in range(1, 16):
        src_t = lax.rem(t + 16 - d, 16)
        arrived(fr.at[src_t], f_r.at[d])
        total += fr[src_t]
    levels_ref[...] = total
    arrived(ob, o_r.at[1])
    states_ref[...] = ob[...]

    for copy in sends:
        copy.wait_send()
    either_sent(rsend, m_s, res_mid)
    for g in range(4):
        either_sent(rmid.at[pl.ds(g * 32, 32)], r_s.at[g], res_dest(g))

    for k in range(8):

        @pl.when(k != pair)
        def _(k=k):
            arrived(yr.at[k], z_s.at[k])

    either_sent(ob_s, o_s.at[0], out_z)
    either_sent(ob_z, o_s.at[1], out_t)


def on_device(q, k, v, res, wo, gain, wm, lw, positions):
    vmem = pl.BlockSpec(memory_space=pltpu.VMEM)
    dma = pltpu.SemaphoreType.DMA
    scratch = [
        pltpu.VMEM((320, TOK), BF16),
        pltpu.VMEM((320,), BF16),
        pltpu.VMEM((320, 128), BF16),
        pltpu.VMEM((8, 128), I32),
        pltpu.VMEM((2, 2, 4, 4, TOK, HD), BF16),
        pltpu.VMEM((320, HD), BF16),
        pltpu.VMEM((256, HD), BF16),
        pltpu.VMEM((256, HD), BF16),
        pltpu.VMEM((64, HD), BF16),
        pltpu.VMEM((64, HD), BF16),
        pltpu.VMEM((320, 128), I32),
        pltpu.VMEM((128, 320), BF16),
        pltpu.VMEM((128, 320), BF16),
        pltpu.VMEM((2, 2, 32, 320), BF16),
        pltpu.VMEM((16, 16, 320), BF16),
        pltpu.VMEM((COLS, 256), BF16),
        pltpu.VMEM((COLS, 320), BF16),
        pltpu.VMEM((COLS, 384), BF16),
        pltpu.VMEM((128, 384), BF16),
        pltpu.VMEM((256, 256), BF16),
        pltpu.VMEM((256, COLS), F32),
        pltpu.VMEM((128, COLS), BF16),
        pltpu.VMEM((128, COLS), BF16),
        pltpu.VMEM((128, COLS), BF16),
        pltpu.VMEM((8, 16, COLS), BF16),
        pltpu.VMEM((256, COLS), BF16),
        pltpu.VMEM((32, 320), BF16),
        pltpu.VMEM((32, 320), BF16),
        pltpu.VMEM((32, 320), BF16),
        pltpu.VMEM((256, 384), BF16),
        pltpu.VMEM((8, 32, 384), BF16),
        pltpu.VMEM((128, 32), F32),
        pltpu.VMEM((16, 8, 32), F32),
        dma((9,)), dma((4,)), dma((4,)), dma((2, 4, 4)), dma((2, 4, 4)), dma((2, 4)), dma((2, 4)), dma((2, 4)), dma((2, 4)),
        dma((16,)), dma((16,)), dma(()), dma(()), dma(()), dma(()), dma((4,)), dma((2, 2)), dma((16,)), dma((16,)), dma((2, 4)), dma((2, 4)),
        dma((8,)), dma((8,)), dma((2,)), dma((2,)), dma((8,)), dma((8,)), dma((8,)), dma((8,)), dma((2,)), dma((2,)), dma((8,)), dma((8,)), dma((16,)), dma((16,)),
    ]
    attended, states, levels = pl.pallas_call(
        kernel,
        out_shape=(
            jax.ShapeDtypeStruct((TOK, 2 * HD), BF16),
            jax.ShapeDtypeStruct((STEPS, 320), BF16),
            jax.ShapeDtypeStruct((8, STEPS), F32),
        ),
        in_specs=[pl.BlockSpec(memory_space=pltpu.HBM)] * 9,
        out_specs=(vmem, vmem, vmem),
        scratch_shapes=scratch,
        compiler_params=pltpu.CompilerParams(
            collective_id=0, has_side_effects=True, vmem_limit_bytes=(54 * 1024 - 256) * 1024
        ),
    )(q, k, v, res.T, wo.T, gain, wm, lw, positions.reshape(8, 128))
    return attended, states, levels.T


def solution(mesh):
    in_specs = (
        P("ctx", "tp"),
        P("ctx", None),
        P("ctx", None),
        P("ctx", "tp"),
        P("tp", "ctx"),
        P("tp"),
        P("ctx", "tp"),
        P("tp", None),
        P(),
    )
    out_specs = (P("ctx", "tp"), P("ctx", "tp"), P("ctx", "tp"))
    return jax.shard_map(
        on_device, mesh=mesh, in_specs=in_specs, out_specs=out_specs, check_vma=False
    )
```

```python
import functools

import jax
import jax.numpy as jnp
from jax import lax
from jax.experimental import pallas as pl
from jax.experimental.pallas import tpu as pltpu
from jax.sharding import PartitionSpec as P

D = 5120
HD = 128
TOK = 128
STEPS = 32
COLS = 640
MASKED = -1e30
MESH = pl.DeviceIdType.MESH
F32 = jnp.float32
BF16 = jnp.bfloat16
I32 = jnp.int32


def iota(shape, dim):
    return lax.broadcasted_iota(I32, shape, dim)


def nn(a, b):
    return lax.dot_general(a, b, (((1,), (0,)), ((), ())), preferred_element_type=F32)


def nt(a, b):
    return lax.dot_general(a, b, (((1,), (1,)), ((), ())), preferred_element_type=F32)


def tn(a, b):
    return lax.dot_general(a, b, (((0,), (0,)), ((), ())), preferred_element_type=F32)


def shift(rows, cols, offset):
    return (iota((rows, cols), 0) + offset == iota((rows, cols), 1)).astype(BF16)


def kernel(
    q_hbm, k_hbm, v_hbm, res_hbm, wo_hbm, gain_hbm, wm_hbm, lw_hbm, pos_hbm,
    att_ref, states_ref, levels_ref,
    res_ref, gain_ref, lw_ref, pos_ref, kv, qall, qsend, qrecv, qmid_s, qmid_r, posc,
    rsend, rmid, rbuf, gbuf, wob, wmb, wmbig, lwt,
    agrp, res_add, pb, px, ph, rb, sb, ob_s, ob_z, ob, yb, yr, fb, fr,
    in_s, far_s, far_r, near_s, near_r, y_s, y_r, c_s, c_r,
    q_s, q_r, qm_s, qm_r, m_s, m_r, r_s, r_r, g_s, g_r, w_s, w_r,
    a_s, a_r, x_s, x_r, p_s, p_r, s_s, s_r, o_s, o_r, z_s, z_r, f_s, f_r,
):
    c = lax.axis_index("ctx")
    t = lax.axis_index("tp")
    z = lax.rem(c, 16)
    yh = c // 16
    core = lax.rem(t, 2)
    group = t // 2
    par = lax.rem(z, 2)
    mate_z = z + 1 - 2 * par
    pair = z // 2
    zr = lax.rem(z, 4)
    zq = z // 4
    partner = ((1 - yh) * 16 + z, t)
    other_core = (c, t + 1 - 2 * core)
    sends = []

    def zdev(d):
        return (yh * 16 + lax.rem(z + 16 + d, 16), t)

    def tdev(d):
        return (c, lax.rem(t + d, 16))

    def send(src, dst, ssem, rsem, dev):
        copy = pltpu.make_async_remote_copy(
            src_ref=src, dst_ref=dst, send_sem=ssem, recv_sem=rsem, device_id=dev, device_id_type=MESH
        )
        copy.start()
        sends.append(copy)

    def elsewhere(dev):
        return jnp.logical_not((dev[0] == c) & (dev[1] == t))

    def either(src, dst, ssem, rsem, dev):
        @pl.when(elsewhere(dev))
        def _():
            pltpu.make_async_remote_copy(
                src_ref=src, dst_ref=dst, send_sem=ssem, recv_sem=rsem, device_id=dev, device_id_type=MESH
            ).start()

        @pl.when(jnp.logical_not(elsewhere(dev)))
        def _():
            pltpu.make_async_copy(src, dst, rsem).start()

    def either_sent(src, ssem, dev):
        @pl.when(elsewhere(dev))
        def _():
            arrived(src, ssem)

    def arrived(dst, rsem):
        pltpu.make_async_copy(dst, dst, rsem).wait()

    barrier = pltpu.get_barrier_semaphore()

    def greet(dev):
        pl.semaphore_signal(barrier, inc=1, device_id=dev, device_id_type=MESH)

    for d in range(1, 16):
        greet(zdev(d))
        greet(tdev(d))
    greet(partner)
    greet(((1 - yh) * 16 + mate_z, t))
    half_t, slot_t = t // 8, lax.rem(t, 8)
    res_mid = (c, lax.rem(yh + half_t, 2) * 8 + lax.rem(slot_t + 64 - 3 * pair, 8))
    held_pair = lax.rem(slot_t + 3 * pair, 8)
    held_half = lax.rem(half_t + yh, 2)
    res_pair = lax.rem(3 * (pair + 8 - slot_t), 8)

    def res_dest(g):
        return ((g // 2) * 16 + 2 * held_pair + g % 2, t)

    def res_source(j):
        return lax.rem(half_t + j, 2)

    res_peers = [res_dest(g) for g in range(4)] + [
        (res_source(j) * 16 + 2 * res_pair + p, t) for j in range(2) for p in range(2)
    ]
    n_peers = 32
    for dev in res_peers:
        n_peers += jnp.where(elsewhere(dev), 1, 0)

        @pl.when(elsewhere(dev))
        def _(dev=dev):
            greet(dev)

    w_here = yh * 2 + par
    wo_rows = pl.ds(pl.multiple_of(w_here * 160, 16), 160)
    lanes = pl.ds(pl.multiple_of(group * HD, HD), HD)
    here = kv.at[core, yh, zr, zq]
    fetches = [
        pltpu.make_async_copy(pos_hbm, pos_ref, in_s.at[0]),
        pltpu.make_async_copy(q_hbm.at[:, pl.ds(0, HD)], qall.at[pl.ds(0, TOK)], in_s.at[1]),
        pltpu.make_async_copy(q_hbm.at[:, pl.ds(HD, HD)], qall.at[pl.ds(160, TOK)], in_s.at[2]),
        pltpu.make_async_copy(res_hbm, res_ref, in_s.at[3]),
        pltpu.make_async_copy(gain_hbm, gain_ref, in_s.at[4]),
        pltpu.make_async_copy(lw_hbm, lw_ref, in_s.at[5]),
        pltpu.make_async_copy(wo_hbm, wob.at[wo_rows], in_s.at[6]),
        pltpu.make_async_copy(wm_hbm, wmb.at[wo_rows], in_s.at[7]),
    ]

    @pl.when(core == 0)
    def _():
        pltpu.make_async_copy(k_hbm.at[:, lanes], here, in_s.at[8]).start()

    @pl.when(core == 1)
    def _():
        pltpu.make_async_copy(v_hbm.at[:, lanes], here, in_s.at[8]).start()

    for fetch in fetches:
        fetch.start()

    fetches[0].wait()
    pos8 = pos_ref[...]
    hi8 = (pos8 >> 6).astype(F32).astype(BF16)
    lo8 = (pos8 & 63).astype(F32).astype(BF16)
    eye128 = shift(128, 128, 0)
    base = c * TOK

    def before(limit):
        hits = jnp.where(pos8 < limit, 1.0, 0.0)
        return jnp.sum(jnp.sum(hits, axis=1, keepdims=True), axis=0, keepdims=True).astype(I32)

    first = before(base)
    selq = jnp.zeros((256, TOK), F32)
    slot_q = iota((256, 128), 0)
    key_q = (((slot_q >> 3) & 1) * 16 + (slot_q >> 4)) * 4 + (slot_q & 3)

    def held_steps(a):
        spot = pos8[a : a + 1]
        step = iota((1, 128), 1) + a * 128
        here_too = (spot >= base) & (spot < base + TOK)
        key = jnp.where(here_too, (step & 31) * 4 + ((step - first) >> 5), -1)
        return key, (spot == iota((TOK, 128), 0) + base).astype(BF16)

    for a in range(8):
        key, held = held_steps(a)
        selq += nt((key == key_q).astype(BF16), held)
    selq = selq.astype(BF16)
    head_row = (iota((256, 128), 0) >> 2) & 1
    fetches[1].wait()
    fetches[2].wait()
    qsend[...] = jnp.where(
        head_row == 0, nn(selq, qall[0:TOK]), nn(selq, qall[160 : 160 + TOK])
    ).astype(BF16)

    def rows_of(count, owner):
        pick = ((iota((count, 8), 0) & 31) >> 2 == iota((count, 8), 1)).astype(BF16)
        spread = nn(pick, hi8) * 64.0 + nn(pick, lo8)
        lane = (iota((count, 128), 0) & 3) * 32 + owner
        return jnp.sum(jnp.where(iota((count, 128), 1) == lane, spread, 0.0), axis=1, keepdims=True)

    pl.semaphore_wait(barrier, n_peers)

    arrived(here, in_s.at[8])

    def kv_block(plane, n, f):
        py = yh if plane == 0 else 1 - yh
        from_z = lax.rem(z + (0, 15, 1, 14)[n] + 16 - 4 * f, 16)
        return kv.at[core, py, lax.rem(from_z, 4), from_z // 4]

    def kv_bundle(plane, n, kind):
        py = yh if plane == 0 else 1 - yh
        return kv.at[kind, py, lax.rem(zr + (0, 3, 1, 2)[n], 4)]

    def kv_pass(plane, f):
        block = kv_block(plane, 0, f)
        if plane == 0:
            if f in (0, 1):
                send(block, block, near_s.at[0, 3, f], near_r.at[0, 3, f], zdev(2))
            if f in (0, 3):
                send(block, block, near_s.at[0, 3, 2 + f // 3], near_r.at[0, 3, 2 + f // 3], zdev(-2))
        for n, d in ((1, 1), (2, -1)):
            send(block, block, near_s.at[plane, n, f], near_r.at[plane, n, f], zdev(d))

    def kv_cross(n, f):
        block = kv_block(0, n, f)
        send(block, block, y_s.at[n // 3, f], y_r.at[n // 3, f], partner)

    def kv_core(plane, n):
        bundle = kv_bundle(plane, n, core)
        send(bundle, bundle, c_s.at[plane, n], c_r.at[plane, n], other_core)

    def weight_rows(r):
        slot = (yh if r < 2 else 1 - yh) * 2 + (par if r % 2 == 0 else 1 - par)
        return pl.ds(pl.multiple_of(slot * 160, 16), 160)

    def weight_send(w, r):
        buffer = (wob, wmb)[w]
        rows = weight_rows(1) if r == 3 else wo_rows
        dev = (yh * 16 + mate_z, t) if r == 1 else partner
        send(buffer.at[rows], buffer.at[rows], w_s.at[w, r], w_r.at[w, r], dev)

    def weight_wait(w, r):
        arrived((wob, wmb)[w].at[weight_rows(r)], w_r.at[w, r])

    for f in (2, 1, 3):
        send(here, here, far_s.at[f], far_r.at[f], zdev(4 * f))
    kv_cross(0, 0)
    for d in (8, 7, 9, 6, 10, 5, 11, 4, 12, 3, 13, 2, 14, 1, 15):
        zd = lax.rem(z + d, 16)
        send(
            qsend.at[pl.ds(zd * 16, 16)], qrecv.at[pl.ds(z * 16, 16)], q_s.at[d], q_r.at[d], zdev(d)
        )
    qrecv[pl.ds(pl.multiple_of(z * 16, 16), 16)] = qsend[pl.ds(pl.multiple_of(z * 16, 16), 16)]
    kv_pass(0, 0)
    fetches[6].wait()
    weight_send(0, 2)
    fetches[7].wait()
    weight_send(1, 2)
    weight_send(0, 1)
    mine = rows_of(STEPS, c)
    for h in range(2):
        posc[h * 160 : h * 160 + TOK] = iota((TOK, 128), 0) + base
        posc[h * 160 + TOK : (h + 1) * 160] = jnp.broadcast_to(mine.astype(I32), (STEPS, 128))
    selr = jnp.zeros((128, TOK), F32)
    slot_r = iota((128, 128), 0)
    key_r = ((slot_r >> 6) * 16 + ((slot_r >> 2) & 7) * 2 + ((slot_r >> 5) & 1)) * 4 + (slot_r & 3)
    for a in range(8):
        key, held = held_steps(a)
        selr += nt((key == key_r).astype(BF16), held)
    fetches[3].wait()
    rsend[...] = nt(selr.astype(BF16), res_ref[...]).astype(BF16)
    fetches[4].wait()
    either(rsend, rmid, m_s, m_r, res_mid)
    gbuf[t] = jnp.broadcast_to(gain_ref[...].astype(F32).reshape(1, 320), (16, 320)).astype(BF16)
    gain_wanted = slot_t == pair

    @pl.when(gain_wanted)
    def _():
        for d in range(1, 16):
            pltpu.make_async_remote_copy(
                src_ref=gbuf.at[t], dst_ref=gbuf.at[t], send_sem=g_s.at[d], recv_sem=g_r.at[half_t],
                device_id=tdev(d), device_id_type=MESH,
            ).start()

    fetches[5].wait()
    lwt[...] = nn(nt(eye128, lw_ref[...]).astype(BF16), shift(320, 384, 0)).astype(BF16)

    arrived(kv_block(1, 0, 0), y_r.at[0, 0])
    kv_pass(1, 0)

    def kv_far(f):
        arrived(kv_block(0, 0, f), far_r.at[f])
        kv_cross(0, f)
        kv_pass(0, f)

    def kv_two(i, f):
        arrived(kv_block(0, 3, f), near_r.at[0, 3, i])
        kv_cross(3, f)

    def kv_other(f):
        arrived(kv_block(1, 0, f), y_r.at[0, f])
        kv_pass(1, f)

    kv_far(1)
    kv_far(3)
    kv_two(0, 0)
    kv_two(2, 3)
    kv_far(2)
    kv_core(0, 0)
    weight_wait(0, 1)
    weight_send(0, 3)

    for d in range(1, 16):
        from_z = lax.rem(z + 16 - d, 16)
        arrived(qrecv.at[pl.ds(from_z * 16, 16)], q_r.at[d])
    lane = iota((STEPS, 256), 1)
    for which in range(2):
        o_y = yh if which == 0 else 1 - yh
        spots = rows_of(STEPS, o_y * 16 + z).astype(I32)
        source = spots >> 7
        diagonal = iota((STEPS, STEPS), 0) == iota((STEPS, STEPS), 1)
        source_row = jnp.sum(
            jnp.where(diagonal, source.astype(F32), 0.0), axis=0, keepdims=True
        ).astype(I32)
        earlier = iota((STEPS, STEPS), 1) < iota((STEPS, STEPS), 0)
        rank = jnp.sum(
            jnp.where((source == source_row) & earlier, 1.0, 0.0), axis=1, keepdims=True
        ).astype(I32)
        for h in range(2):
            wanted = (source & 15) * 16 + o_y * 8 + h * 4 + rank
            take = ((wanted == lane) & (source >> 4 == yh)).astype(BF16)
            rows = nn(take, qrecv[...]).astype(BF16)
            if which == 0:
                qall[h * 160 + TOK : (h + 1) * 160] = rows
            else:
                qmid_s[h * STEPS : (h + 1) * STEPS] = rows
    send(qmid_s, qmid_r, qm_s, qm_r, partner)

    state = [jnp.full((320, 1), MASKED, F32), jnp.zeros((320, 1), F32), jnp.zeros((320, HD), F32)]

    def attend(p, n):
        py = yh if p == 0 else 1 - yh
        set_ = lax.rem(zr + (0, 3, 1, 2)[n], 4)
        arrived(kv_bundle(p, n, 1 - core), c_r.at[p, n])
        keys = kv[0, py, set_].reshape(512, HD)
        values = kv[1, py, set_].reshape(512, HD)
        highest, totals, accum = state
        scores = nt(qall[...], keys) * (HD**-0.5)
        kk = iota((320, 512), 1)
        spot = (py * 16 + set_) * TOK + (kk >> 7) * 512 + (kk & 127)
        scores = jnp.where(spot <= posc[:, 0:1], scores, MASKED)
        new = jnp.maximum(highest, jnp.max(scores, axis=1, keepdims=True))
        alpha = jnp.exp(highest - new)
        weights = jnp.exp(scores - new)
        state[0] = new
        state[1] = totals * alpha + jnp.sum(weights, axis=1, keepdims=True)
        state[2] = accum * alpha + nn(weights.astype(BF16), values)

    kv_other(1)
    kv_other(3)
    kv_two(1, 1)
    kv_two(3, 2)
    kv_core(0, 3)
    kv_other(2)
    kv_core(1, 0)
    arrived(qmid_r, qm_r)
    for h in range(2):
        rows = slice(h * 160 + TOK, (h + 1) * 160)
        qall[rows] = (
            qall[rows].astype(F32) + qmid_r[h * STEPS : (h + 1) * STEPS].astype(F32)
        ).astype(BF16)
    arrived(rmid, m_r)
    for g in range(4):
        either(rmid.at[pl.ds(g * 32, 32)], rbuf.at[held_half, par], r_s.at[g], r_r.at[held_half, par], res_dest(g))

    attend(0, 0)
    for n in (1, 2):
        for f in range(4):
            arrived(kv_block(0, n, f), near_r.at[0, n, f])
        kv_core(0, n)
    attend(1, 0)
    attend(0, 3)
    for n in (1, 2):
        for f in range(4):
            arrived(kv_block(1, n, f), near_r.at[1, n, f])
        kv_core(1, n)

    weight_send(1, 1)
    for bundle in ((0, 1), (0, 2), (1, 1)):
        attend(*bundle)
    for f in range(4):
        arrived(kv_block(1, 3, f), y_r.at[1, f])
    kv_core(1, 3)
    attend(1, 2)
    attend(1, 3)
    mixed = (state[2] / state[1]).astype(BF16)
    k_rows = pl.ds(pl.multiple_of(pair * STEPS, STEPS), STEPS)
    for h in range(2):
        agrp[k_rows, h * HD : (h + 1) * HD] = mixed[h * 160 + TOK : (h + 1) * 160]

    for d in (4, 3, 5, 2, 6, 1, 7):
        send(agrp.at[k_rows], agrp.at[k_rows], a_s.at[d], a_r.at[d], zdev(2 * d))
    for h in range(2):
        att_ref[:, h * HD : (h + 1) * HD] = mixed[h * 160 : h * 160 + TOK]

    weight_wait(1, 1)
    weight_send(1, 3)
    for j in range(2):

        @pl.when(t != j * 8 + pair)
        def _(j=j):
            arrived(gbuf.at[j * 8 + pair], g_r.at[j])

    gain = nn(gbuf[pair], shift(320, COLS, 0)) + nn(gbuf[8 + pair], shift(320, COLS, 320))
    gain = gain[0:1]
    for j in range(2):
        for s in range(2):
            arrived(rbuf.at[j, s], r_r.at[j, s])
    row = iota((256, 1), 0)
    spots = rows_of(256, yh * 16 + 2 * (iota((256, 128), 0) >> 5) + par).astype(I32)
    step = (row & 31) * 32 + yh * 16 + 2 * (row >> 5) + par
    slot = iota((256, 64), 1)
    res_part = jnp.zeros((256, COLS), F32)
    for j in range(2):
        source = res_source(j) * 16 + 2 * res_pair
        nth = (spots >> 7) - source
        rank = (step - jnp.where(nth == 0, before(source * TOK), before((source + 1) * TOK))) >> 5
        wanted = jnp.where((nth == 0) | (nth == 1), nth * 32 + (row >> 5) * 4 + rank, 1000)
        rows = nn((wanted == slot).astype(BF16), rbuf[j].reshape(64, 320)).astype(BF16)
        res_part += nn(rows, shift(320, COLS, j * 320))

    res_add[...] = res_part

    weight_wait(0, 2)
    weight_wait(0, 3)
    for d in range(1, 8):
        from_k = lax.rem(pair + 8 - d, 8)
        arrived(agrp.at[pl.ds(pl.multiple_of(from_k * STEPS, STEPS), STEPS)], a_r.at[d])
    mine = pl.ds(pl.multiple_of(core * 128, 128), 128)
    theirs = pl.ds(pl.multiple_of((1 - core) * 128, 128), 128)
    chip = t // 2
    pb[...] = (nt(agrp[theirs], wob[...]) + res_add[theirs]).astype(BF16)
    send(pb, px, x_s.at[0], x_r.at[0], other_core)
    partial = nt(agrp[mine], wob[...]) + res_add[mine]
    arrived(px, x_r.at[0])
    ph[...] = (partial + px[...].astype(F32)).astype(BF16)

    def chip_rows(index):
        return pl.ds(pl.multiple_of(index * 16, 16), 16)

    for d in (4, 3, 5, 2, 6, 1, 7):
        send(ph.at[chip_rows(lax.rem(chip + d, 8))], rb.at[chip], p_s.at[d], p_r.at[d], tdev(2 * d))
    weight_wait(1, 2)
    weight_wait(1, 3)
    wmbig[...] = nn(wmb[...], shift(320, 384, 0)).astype(BF16)
    total = ph[chip_rows(chip)].astype(F32)
    for d in range(1, 8):
        src = lax.rem(chip + 8 - d, 8)
        arrived(rb.at[src], p_r.at[d])
        total += rb[src].astype(F32)
    own_rows = chip_rows(core * 8 + chip)
    sb[own_rows] = total.astype(BF16)
    for d in (4, 3, 5, 2, 6, 1, 7):
        send(sb.at[own_rows], sb.at[own_rows], s_s.at[d], s_r.at[d], tdev(2 * d))
    for d in range(1, 8):
        arrived(sb.at[chip_rows(core * 8 + lax.rem(chip + 8 - d, 8))], s_r.at[d])
    send(sb.at[mine], sb.at[mine], x_s.at[1], x_r.at[1], other_core)

    def score(rows, first_owner):
        states = sb[rows].astype(F32)
        squares = jnp.sum(states * states, axis=1, keepdims=True)
        pre = nn((states * gain).astype(BF16), wmbig[...])
        sq_hi = squares.astype(BF16).astype(F32)
        col = iota((128, 384), 1)
        pre = jnp.where(col == 320, sq_hi, jnp.where(col == 321, squares - sq_hi, pre))
        yb[rows] = pre.astype(BF16)
        nearby = pair // 4 == first_owner // 4
        for far, near in ((0, 2), (1, 3), (3, 1), (2, 0)):
            k = first_owner + lax.rem(pair + jnp.where(nearby, near, far), 4)
            piece = yb.at[pl.ds(pl.multiple_of(k * STEPS, STEPS), STEPS)]

            @pl.when(k != pair)
            def _(k=k, piece=piece):
                pltpu.make_async_remote_copy(
                    src_ref=piece, dst_ref=yr.at[pair], send_sem=z_s.at[k], recv_sem=z_r.at[pair],
                    device_id=(yh * 16 + 2 * k + par, t), device_id_type=MESH,
                ).start()

    score(mine, core * 4)
    arrived(sb.at[theirs], x_r.at[1])
    score(theirs, (1 - core) * 4)

    out_k = lax.rem(slot_t + 3 * pair, 8)
    block = sb[pl.ds(pl.multiple_of(out_k * STEPS, STEPS), STEPS)]
    ob_s[...] = nn(
        block, (iota((COLS, 320), 0) == iota((COLS, 320), 1) + half_t * 320).astype(BF16)
    ).astype(BF16)

    out_z = (yh * 16 + 2 * out_k + par, t)
    out_t = (c, half_t * 8 + lax.rem(3 * (pair + 8 - slot_t), 8))
    either(ob_s, ob_z, o_s.at[0], o_r.at[0], out_z)

    yr[pair] = yb[k_rows]
    for k in range(8):

        @pl.when(k != pair)
        def _(k=k):
            arrived(yr.at[k], z_r.at[k])

    total = yr[0].astype(F32)
    for k in range(1, 8):
        total += yr[k].astype(F32)
    col = iota((STEPS, 384), 1)
    squares = jnp.sum(jnp.where((col == 320) | (col == 321), total, 0.0), axis=1, keepdims=True)
    pre = jnp.where(col < 320, total * lax.rsqrt(squares / D + 1e-06), 0.0)
    hidden = (pre / (1.0 + jnp.exp(-pre))).astype(BF16)
    fb[...] = nt(lwt[...], hidden)
    for d in range(1, 16):
        to_t = lax.rem(t + d, 16)
        send(fb.at[pl.ds(pl.multiple_of(to_t * 8, 8), 8)], fr.at[t], f_s.at[d], f_r.at[d], tdev(d))
    arrived(ob_z, o_r.at[0])
    either(ob_z, ob, o_s.at[1], o_r.at[1], out_t)
    total = fb[pl.ds(pl.multiple_of(t * 8, 8), 8)]
    for d in range(1, 16):
        src_t = lax.rem(t + 16 - d, 16)
        arrived(fr.at[src_t], f_r.at[d])
        total += fr[src_t]
    levels_ref[...] = total
    arrived(ob, o_r.at[1])
    states_ref[...] = ob[...]

    for copy in sends:
        copy.wait_send()

    @pl.when(gain_wanted)
    def _():
        for d in range(1, 16):
            arrived(gbuf.at[t], g_s.at[d])

    either_sent(rsend, m_s, res_mid)
    for g in range(4):
        either_sent(rmid.at[pl.ds(g * 32, 32)], r_s.at[g], res_dest(g))

    for k in range(8):

        @pl.when(k != pair)
        def _(k=k):
            arrived(yr.at[k], z_s.at[k])

    either_sent(ob_s, o_s.at[0], out_z)
    either_sent(ob_z, o_s.at[1], out_t)


def on_device(q, k, v, res, wo, gain, wm, lw, positions):
    vmem = pl.BlockSpec(memory_space=pltpu.VMEM)
    dma = pltpu.SemaphoreType.DMA
    scratch = [
        pltpu.VMEM((320, TOK), BF16),
        pltpu.VMEM((320,), BF16),
        pltpu.VMEM((320, 128), BF16),
        pltpu.VMEM((8, 128), I32),
        pltpu.VMEM((2, 2, 4, 4, TOK, HD), BF16),
        pltpu.VMEM((320, HD), BF16),
        pltpu.VMEM((256, HD), BF16),
        pltpu.VMEM((256, HD), BF16),
        pltpu.VMEM((64, HD), BF16),
        pltpu.VMEM((64, HD), BF16),
        pltpu.VMEM((320, 128), I32),
        pltpu.VMEM((128, 320), BF16),
        pltpu.VMEM((128, 320), BF16),
        pltpu.VMEM((2, 2, 32, 320), BF16),
        pltpu.VMEM((16, 16, 320), BF16),
        pltpu.VMEM((COLS, 256), BF16),
        pltpu.VMEM((COLS, 320), BF16),
        pltpu.VMEM((COLS, 384), BF16),
        pltpu.VMEM((128, 384), BF16),
        pltpu.VMEM((256, 256), BF16),
        pltpu.VMEM((256, COLS), F32),
        pltpu.VMEM((128, COLS), BF16),
        pltpu.VMEM((128, COLS), BF16),
        pltpu.VMEM((128, COLS), BF16),
        pltpu.VMEM((8, 16, COLS), BF16),
        pltpu.VMEM((256, COLS), BF16),
        pltpu.VMEM((32, 320), BF16),
        pltpu.VMEM((32, 320), BF16),
        pltpu.VMEM((32, 320), BF16),
        pltpu.VMEM((256, 384), BF16),
        pltpu.VMEM((8, 32, 384), BF16),
        pltpu.VMEM((128, 32), F32),
        pltpu.VMEM((16, 8, 32), F32),
        dma((9,)), dma((4,)), dma((4,)), dma((2, 4, 4)), dma((2, 4, 4)), dma((2, 4)), dma((2, 4)), dma((2, 4)), dma((2, 4)),
        dma((16,)), dma((16,)), dma(()), dma(()), dma(()), dma(()), dma((4,)), dma((2, 2)), dma((16,)), dma((16,)), dma((2, 4)), dma((2, 4)),
        dma((8,)), dma((8,)), dma((2,)), dma((2,)), dma((8,)), dma((8,)), dma((8,)), dma((8,)), dma((2,)), dma((2,)), dma((8,)), dma((8,)), dma((16,)), dma((16,)),
    ]
    attended, states, levels = pl.pallas_call(
        kernel,
        out_shape=(
            jax.ShapeDtypeStruct((TOK, 2 * HD), BF16),
            jax.ShapeDtypeStruct((STEPS, 320), BF16),
            jax.ShapeDtypeStruct((8, STEPS), F32),
        ),
        in_specs=[pl.BlockSpec(memory_space=pltpu.HBM)] * 9,
        out_specs=(vmem, vmem, vmem),
        scratch_shapes=scratch,
        compiler_params=pltpu.CompilerParams(
            collective_id=0, has_side_effects=True, vmem_limit_bytes=(54 * 1024 - 256) * 1024
        ),
    )(q, k, v, res.T, wo.T, gain, wm, lw, positions.reshape(8, 128))
    return attended, states, levels.T


def solution(mesh):
    in_specs = (
        P("ctx", "tp"),
        P("ctx", None),
        P("ctx", None),
        P("ctx", "tp"),
        P("tp", "ctx"),
        P("tp"),
        P("ctx", "tp"),
        P("tp", None),
        P(),
    )
    out_specs = (P("ctx", "tp"), P("ctx", "tp"), P("ctx", "tp"))
    return jax.shard_map(
        on_device, mesh=mesh, in_specs=in_specs, out_specs=out_specs, check_vma=False
    )
```
